512 devices in a mesh: seq: 16 (over y, x), mem: 32 (over z, core).
Axes of the slice: x: 4, y: 4, z: 16, core: 2. Of those that a mesh axis runs over, the one named last changes fastest.
Arguments:
- query: bfloat16 [65536, 2048], P(('seq', 'mem')), may hold values from -64 to 64
- key: bfloat16 [65536, 2048], P(('seq', 'mem')), may hold values from -64 to 64
- value: bfloat16 [65536, 2048], P(('seq', 'mem')), may hold values from -6 to 6
- mem_key: bfloat16 [4096, 2048], P('mem'), may hold values from -6 to 6
- mem_value: bfloat16 [4096, 2048], P('mem'), may hold values from -6 to 6
- block_ids: int32 [8192, 2], P(('seq', 'mem')), may hold values from 0 to 31, all different within a row; in each aligned block of 16 rows (0 to 15, 16 to 31, ...) at most 2 rows name the same one
- gate_logit: float32 [16], replicated, may hold values from -2 to 2
- d_out: bfloat16 [65536, 2048], P(('seq', 'mem')), may hold values from -16 to 16
Outputs:
- out: bfloat16 [65536, 2048], P(('seq', 'mem'))
- d_query: bfloat16 [65536, 2048], P(('seq', 'mem'))
- gate_grad: float32 [16], replicated
The draws below stay inside these ranges and needn't reach their ends.
Inputs may be any that keep to these rules, and one draw needn't show every extreme that they name: `block_ids`: each row names 2 different memory blocks. Among the query groups of one device no block is named by more than 2 rows, and some device names some block exactly 2 times.
All inputs are finite; a program needn't handle non-finite values.
Results may differ from the reference program's by a relative error of at most 0.015.
Values may be sent and summed in bfloat16 or wider, within the bound.
A program may use at most 64 MiB of HBM per device.

```python
import math
import jax
import jax.numpy as jnp
import numpy as np
from jax import lax

HEADS = 16
HEAD_DIM = 128
QBLK = 8
TOPB = 2
MROWS = 128
T_DEV = 128
WIDTH = 2048
TOKENS = 65536
NQG = 8192
MEM_ROWS = 4096
CAP = 2
N_MEM = 32


def draw_query(key, part):
    key = jax.random.fold_in(key, 7)
    drawn = jax.random.normal(key, (TOKENS, HEADS * HEAD_DIM), jnp.float32)
    return jnp.clip(drawn, -64.0, 64.0).astype(jnp.bfloat16)


def draw_key(key, part):
    key = jax.random.fold_in(key, 8)
    drawn = jax.random.normal(key, (TOKENS, HEADS * HEAD_DIM), jnp.float32)
    return jnp.clip(drawn, -64.0, 64.0).astype(jnp.bfloat16)


def draw_d_out(key, part):
    key = jax.random.fold_in(key, 9)
    rows_all = jnp.arange(TOKENS).astype(jnp.float32) / TOKENS
    drawn = jnp.clip(jax.random.normal(key, (TOKENS, HEADS * HEAD_DIM), jnp.float32), -5.0, 5.0)
    drawn = drawn * (3.0 ** rows_all)[:, None]
    return drawn.astype(jnp.bfloat16)


def levels(rng, dims, pieces, smallest, top_value):
    level = 1.0
    for position, parts in pieces:
        heights = jax.random.uniform(jax.random.fold_in(jax.random.fold_in(rng, 6), position), (parts,), jnp.float32, smallest / len(pieces), top_value / len(pieces))
        level = level * jnp.repeat(jnp.exp(heights), dims[position] // parts).reshape((-1,) + (1,) * (len(dims) - 1 - position))
    return level


def shared_out(rng, own, number, rows, amount, top, reach, lean):
    sequence = jax.random.permutation(rng, amount)
    heavy_load, common = shares(amount, rows * top, reach, lean, True), shares(amount, rows * top, reach, lean, False)
    places = jnp.arange(amount)

    def named(tallies, turn):
        used = int((tallies > 0).sum())
        fixed = max(1, used // 4)
        shifted = fixed + (places - fixed + turn * (used - fixed)) % max(1, amount - fixed)
        return jnp.zeros((amount,), jnp.int32).at[sequence[jnp.where(places < fixed, places, shifted)]].set(jnp.asarray(tallies, jnp.int32))

    tallies = jnp.where(number % 4 == 0, named(heavy_load, number // 4), named(common, number - number // 4 - 1))
    mixed = jax.random.permutation(jax.random.fold_in(own, 3), amount)
    giver, sink = mixed[0:amount // 2 * 2:2], mixed[1:amount // 2 * 2:2]
    room = jnp.minimum(tallies[giver] - 1, reach - tallies[sink]) // 2
    room = jnp.where((giver == sequence[0]) | (sink == sequence[0]) | (tallies[sink] == 0), 0, jnp.maximum(room, 0))
    shifted = jax.random.randint(jax.random.fold_in(own, 4), (amount // 2,), 0, 1 << 20) % (room + 1)
    tallies = tallies.at[giver].add(-shifted).at[sink].add(shifted)
    items = jnp.searchsorted(jnp.cumsum(tallies), jnp.arange(rows * top), side="right").astype(jnp.int32)
    table = items.reshape(top, rows).T
    table = table[jax.random.permutation(jax.random.fold_in(own, 1), rows)]
    turn = jax.random.randint(jax.random.fold_in(own, 2), (rows, 1), 0, top)
    return jnp.take_along_axis(table, (jnp.arange(top)[None, :] + turn) % top, axis=1)


def shares(amount, total, bound, lean, full):
    loads = [(1 << 20) // math.isqrt(grade ** lean) + 1 for grade in range(1, amount + 1)]
    largest = bound if full else min(bound, max(-(-total // amount), total * loads[0] // sum(loads)))
    least = 1 if total - largest >= amount - 1 else 0
    counts, surplus = [largest] + [least] * (amount - 1), total - largest - least * (amount - 1)
    while surplus > 0:
        free = [i for i in range(1, amount) if counts[i] < largest] or [i for i in range(1, amount) if counts[i] < bound]
        mass, budget = sum([loads[i] for i in free]), surplus
        for i in free:
            extra = min(bound - counts[i], max(1, budget * loads[i] // mass), surplus)
            counts[i] = counts[i] + extra
            surplus = surplus - extra
    return np.array(counts)


def scatter_about(key, extent, deviation, bound, shards=(), kind=jnp.bfloat16):
    entries = jax.random.normal(key, extent, jnp.float32) * deviation
    if len(shards) > 0:
        entries = levels(key, extent, shards, -0.22, 0.18) * entries
    return jnp.clip(entries, min=-bound, max=bound).astype(kind)


def setup_inputs(seed: int = 0) -> dict:
    key_of = jax.random.split(jax.random.key(seed), 9)
    query = draw_query(jax.random.fold_in(key_of[8], 71), 0)
    key = draw_key(jax.random.fold_in(key_of[8], 71), 0)
    value = scatter_about(key_of[2], (TOKENS, WIDTH), 1.0, 6.0, ((0, 512),))
    mem_key = scatter_about(key_of[3], (MEM_ROWS, WIDTH), 1.0, 6.0, ((0, 32),))
    mem_value = scatter_about(key_of[4], (MEM_ROWS, WIDTH), 1.0, 6.0, ((0, 32),))
    block_ids_keys = jax.random.split(jax.random.fold_in(key_of[5], 1), NQG // (T_DEV // QBLK))
    block_ids_turns = jax.random.permutation(jax.random.fold_in(key_of[5], 3), NQG // (T_DEV // QBLK))
    block_ids = jax.vmap(lambda own, number: shared_out(jax.random.fold_in(key_of[5], 2), own, number, T_DEV // QBLK, N_MEM, TOPB, CAP, 2))(block_ids_keys, block_ids_turns).reshape((NQG, TOPB))
    gate_logit = jnp.clip(jax.random.uniform(key_of[6], (HEADS,), jnp.float32, -2.0, 2.0), -2.0, 2.0)
    d_out = draw_d_out(jax.random.fold_in(key_of[8], 71), 0)
    return dict(query=query, key=key, value=value, mem_key=mem_key, mem_value=mem_value, block_ids=block_ids, gate_logit=gate_logit, d_out=d_out)


def reference(query, key, value, mem_key, mem_value, block_ids, gate_logit, d_out):
    softmax_scale = HEAD_DIM ** (-0.5)
    groups = T_DEV // QBLK
    block_count = TOKENS // T_DEV
    gate_open = jax.nn.sigmoid(gate_logit.astype(jnp.float32))
    gate_col = gate_open[None, :, None]
    mem_k_blocks = mem_key.reshape(N_MEM, MROWS, HEADS, HEAD_DIM)
    mem_v_blocks = mem_value.reshape(N_MEM, MROWS, HEADS, HEAD_DIM)
    rows_idx = lax.broadcasted_iota(jnp.int32, (T_DEV, T_DEV), 0)
    cols_idx = lax.broadcasted_iota(jnp.int32, (T_DEV, T_DEV), 1)
    causal_mask = rows_idx >= cols_idx

    def one_block(inputs):
        q_block, k_block, v_block, g_block, id_block = inputs
        q_heads = q_block.reshape(T_DEV, HEADS, HEAD_DIM).astype(jnp.float32)
        k_heads = k_block.reshape(T_DEV, HEADS, HEAD_DIM).astype(jnp.float32)
        v_heads = v_block.reshape(T_DEV, HEADS, HEAD_DIM).astype(jnp.float32)
        grad_f = g_block.reshape(T_DEV, HEADS, HEAD_DIM).astype(jnp.float32)
        local_scores = jnp.einsum('qhd,khd->hqk', q_heads, k_heads) * softmax_scale
        local_scores = jnp.where(causal_mask[None], local_scores, -1e+30)
        local_peak = lax.optimization_barrier(jnp.max(local_scores, axis=-1, keepdims=True))
        local_exp = jnp.exp(local_scores - local_peak)
        local_prob = local_exp / lax.optimization_barrier(jnp.sum(local_exp, axis=-1, keepdims=True))
        local_weight = lax.optimization_barrier(local_prob.astype(jnp.bfloat16)).astype(jnp.float32)
        local_out = jnp.einsum('hqk,khd->qhd', local_weight, v_heads)
        picked_k = mem_k_blocks[id_block].astype(jnp.float32)
        picked_v = mem_v_blocks[id_block].astype(jnp.float32)
        q_groups = q_heads.reshape(groups, QBLK, HEADS, HEAD_DIM)
        pair_scores = jnp.einsum('gqhd,gtkhd->gthqk', q_groups, picked_k) * softmax_scale
        pair_peak = lax.optimization_barrier(jnp.max(pair_scores, axis=-1, keepdims=True))
        pair_lse = pair_peak + jnp.log(lax.optimization_barrier(jnp.sum(jnp.exp(pair_scores - pair_peak), axis=-1, keepdims=True)))
        pair_weight = lax.optimization_barrier(jnp.exp(pair_scores - pair_lse).astype(jnp.bfloat16)).astype(jnp.float32)
        pair_out = jnp.einsum('gthqk,gtkhd->gtqhd', pair_weight, picked_v)
        pair_out = lax.optimization_barrier(pair_out.astype(jnp.bfloat16)).astype(jnp.float32)
        lse_peak = lax.optimization_barrier(jnp.max(pair_lse, axis=1, keepdims=True))
        total_lse = lse_peak + jnp.log(lax.optimization_barrier(jnp.sum(jnp.exp(pair_lse - lse_peak), axis=1, keepdims=True)))
        pair_share = jnp.exp(pair_lse - total_lse)
        share_view = jnp.transpose(pair_share[..., 0], (0, 1, 3, 2))[..., None]
        mem_out = lax.optimization_barrier(jnp.sum(share_view * pair_out, axis=1)).reshape(T_DEV, HEADS, HEAD_DIM)
        mixed = gate_col * mem_out + (1.0 - gate_col) * local_out
        out_block = mixed.astype(jnp.bfloat16).reshape(T_DEV, HEADS * HEAD_DIM)
        gate_term = lax.optimization_barrier(jnp.sum(grad_f * (mem_out - local_out), axis=(0, 2)))
        local_dout = lax.optimization_barrier(((1.0 - gate_col) * grad_f).astype(jnp.bfloat16)).astype(jnp.float32)
        local_delta = lax.optimization_barrier(jnp.sum(local_dout * local_out, axis=-1))
        local_dp = jnp.einsum('qhd,khd->hqk', local_dout, v_heads)
        local_ds = local_prob * (local_dp - jnp.transpose(local_delta)[:, :, None])
        local_ds = lax.optimization_barrier(local_ds.astype(jnp.bfloat16)).astype(jnp.float32)
        local_dq = jnp.einsum('hqk,khd->qhd', local_ds, k_heads) * softmax_scale
        mem_dout = lax.optimization_barrier((gate_col * grad_f).astype(jnp.bfloat16)).astype(jnp.float32)
        mem_delta = lax.optimization_barrier(jnp.sum(mem_dout * mem_out, axis=-1))
        dout_groups = mem_dout.reshape(groups, QBLK, HEADS, HEAD_DIM)
        delta_view = jnp.transpose(mem_delta.reshape(groups, QBLK, HEADS), (0, 2, 1))[:, None, :, :, None]
        pair_prob = jnp.exp(pair_scores - total_lse)
        pair_dp = jnp.einsum('gqhd,gtkhd->gthqk', dout_groups, picked_v)
        mem_ds = lax.optimization_barrier((pair_prob * (pair_dp - delta_view)).astype(jnp.bfloat16)).astype(jnp.float32)
        pair_dq = jnp.einsum('gthqk,gtkhd->gtqhd', mem_ds, picked_k) * softmax_scale
        pair_dq = lax.optimization_barrier(pair_dq.astype(jnp.bfloat16)).astype(jnp.float32)
        mem_dq = lax.optimization_barrier(jnp.sum(pair_dq, axis=1)).reshape(T_DEV, HEADS, HEAD_DIM)
        dq_block = (local_dq + mem_dq).astype(jnp.bfloat16).reshape(T_DEV, HEADS * HEAD_DIM)
        return (out_block, dq_block, gate_term)
    stacked = (query.reshape(block_count, T_DEV, HEADS * HEAD_DIM), key.reshape(block_count, T_DEV, HEADS * HEAD_DIM), value.reshape(block_count, T_DEV, HEADS * HEAD_DIM), d_out.reshape(block_count, T_DEV, HEADS * HEAD_DIM), block_ids.reshape(block_count, groups, TOPB).astype(jnp.int32))
    out_blocks, dq_blocks, gate_terms = lax.map(one_block, stacked)
    gate_grad = lax.optimization_barrier(jnp.sum(gate_terms, axis=0)) * gate_open * (1.0 - gate_open) / math.sqrt(TOKENS)
    out = out_blocks.reshape(TOKENS, HEADS * HEAD_DIM)
    d_query = dq_blocks.reshape(TOKENS, HEADS * HEAD_DIM)
    return (out, d_query, gate_grad)
```

```python
import functools
import math

import jax
import jax.numpy as jnp
from jax import lax
from jax.experimental import pallas as pl
from jax.experimental.pallas import tpu as pltpu
from jax.sharding import PartitionSpec as P

NX = 4
MESH = pl.DeviceIdType.MESH
HD = 128
F32 = jnp.float32
BF16 = jnp.bfloat16


def dot_nt(a, b):
    return lax.dot_general(a, b, (((1,), (1,)), ((), ())), preferred_element_type=F32)


def dot_nn(a, b):
    return jnp.dot(a, b, preferred_element_type=F32)


def kernel(
    nz, total_tokens,
    q_hbm, k_hbm, v_hbm, mk_hbm, mv_hbm, d_hbm, ids_ref, gl_ref,
    out_hbm, dq_hbm, gg_ref,
    kb, vb, qs, ks, vs, gs, md, qg, mg, po, da, db, ls, dl, lo, ldq, so, sd, gx, codes, codes_sm,
    rc, rx, ry, rz,
    loc, swap_s, swap_r, res_s, res_r,
    zk_s, zk_r, zv_s, zv_r,
    xa_s, xa_r, xb_s, xb_r, xc_s, xc_r, xd_s, xd_r,
    ya_s, ya_r, yb_s, yb_r, yc_s, yc_r, yd_s, yd_r,
    rc_s, rc_r, rx_s, rx_r, ry_s, ry_r, rz_s, rz_r,
):
    rows = q_hbm.shape[0]
    half = q_hbm.shape[1] // 2
    heads = half // HD
    groups = ids_ref.shape[0]
    gr = rows // groups
    quarter = 2 * rows // NX
    eighth = quarter // 2
    scale = HD ** -0.5

    s = lax.axis_index("seq")
    m = lax.axis_index("mem")
    x, y = lax.rem(s, NX), s // NX
    z, c = m // 2, lax.rem(m, 2)
    other = 1 - c

    def at_x(step):
        return (y * NX + lax.rem(x + step + NX, NX), m)

    def at_y(step):
        return (lax.rem(y + step + NX, NX) * NX + x, m)

    def at_z(step):
        return (s, lax.rem(z + step + nz, nz) * 2 + c)

    sib = (s, z * 2 + other)

    mine = pl.ds(pl.multiple_of(c * half, half), half)
    theirs = pl.ds(pl.multiple_of(other * half, half), half)
    my_rows = pl.ds(pl.multiple_of(c * rows, rows), rows)
    sib_rows = pl.ds(pl.multiple_of(other * rows, rows), rows)

    pairs = [(mk_hbm, kb.at[z]), (mv_hbm, vb.at[z]), (q_hbm, qs), (d_hbm, gs), (k_hbm, ks), (v_hbm, vs)]
    own = [
        pltpu.make_async_copy(src.at[:, mine], dst.at[my_rows], loc.at[i])
        for i, (src, dst) in enumerate(pairs)
    ]
    for cp in own:
        cp.start()

    barrier = pltpu.get_barrier_semaphore()

    def greet(dev):
        pl.semaphore_signal(barrier, inc=1, device_id=dev, device_id_type=MESH)

    greet(sib)
    for step in range(1, NX):
        greet(at_x(step))
        greet(at_y(step))

    def greet_z(step, carry):
        greet(at_z(step))
        return carry

    lax.fori_loop(1, nz, greet_z, 0)

    a0 = jnp.broadcast_to(ids_ref[:, 0:1], (groups, rows))
    a1 = jnp.broadcast_to(ids_ref[:, 1:2], (groups, rows))
    g_row = lax.broadcasted_iota(jnp.int32, (groups, rows), 0)
    g_tok = lax.broadcasted_iota(jnp.int32, (groups, rows), 1) // gr
    zero = jnp.zeros((groups, rows), jnp.int32)
    here = g_row == g_tok
    i0 = jnp.sum(jnp.where(here, a0, zero), axis=0, keepdims=True)
    i1 = jnp.sum(jnp.where(here, a1, zero), axis=0, keepdims=True)
    one = zero + 1
    earlier = g_row < g_tok
    r0 = jnp.sum(jnp.where(earlier & ((a0 == i0) | (a1 == i0)), one, zero), axis=0, keepdims=True)
    r1 = jnp.sum(jnp.where(earlier & ((a0 == i1) | (a1 == i1)), one, zero), axis=0, keepdims=True)
    code0 = i0 * 4 + c * 2 + r0
    code1 = i1 * 4 + c * 2 + r1
    first = lax.broadcasted_iota(jnp.int32, (8, rows), 0) == 0
    codes[c] = jnp.where(first, jnp.broadcast_to(code0, (8, rows)), jnp.broadcast_to(code1, (8, rows)))

    for j in range(heads):
        logit = jnp.full((8, HD), gl_ref[c * heads + j], F32)
        gx[:, j * HD:(j + 1) * HD] = 1.0 / (1.0 + jnp.exp(-logit))

    pl.semaphore_wait(barrier, 1 + 2 * (NX - 1) + nz - 1)

    swaps = [
        pltpu.make_async_remote_copy(
            src_ref=src.at[:, theirs], dst_ref=dst.at[my_rows],
            send_sem=swap_s.at[i], recv_sem=swap_r.at[i], device_id=sib, device_id_type=MESH,
        )
        for i, (src, dst) in enumerate(pairs)
    ]
    code_swap = pltpu.make_async_remote_copy(
        src_ref=codes.at[c], dst_ref=codes.at[c],
        send_sem=swap_s.at[6], recv_sem=swap_r.at[6], device_id=sib, device_id_type=MESH,
    )
    swaps[0].start()
    swaps[1].start()
    code_swap.start()
    for cp in swaps[2:]:
        cp.start()

    def got_swap(i):
        own[i].wait()
        pltpu.make_async_remote_copy(
            src_ref=pairs[i][0].at[:, mine], dst_ref=pairs[i][1].at[sib_rows],
            send_sem=swap_s.at[i], recv_sem=swap_r.at[i], device_id=sib, device_id_type=MESH,
        ).wait_recv()

    def part(buf, o, row, count):
        return buf.at[o, pl.ds(pl.multiple_of(row, count), count)]

    def push(buf, o, row, count, send, recv, dev):
        return pltpu.make_async_remote_copy(
            src_ref=part(buf, o, row, count), dst_ref=part(buf, o, row, count),
            send_sem=send, recv_sem=recv, device_id=dev, device_id_type=MESH,
        )

    def k_z(o, j, step):
        return push(kb, o, x * quarter, quarter, zk_s.at[j], zk_r.at[j], at_z(step))

    def v_z(o, j, step):
        return push(vb, o, y * quarter, quarter, zv_s.at[j], zv_r.at[j], at_z(step))

    def origin(n):
        away = (n + 1) // 2
        return lax.rem(z + nz + jnp.where(lax.rem(n, 2) == 1, -away, away), nz)

    last = nz - 1

    def forward_z(n, o):
        odd = lax.rem(n, 2) == 1

        @pl.when(odd & (n + 2 <= last))
        def _():
            k_z(o, n + 2, 1).start()

        @pl.when(odd & (n + 2 < last))
        def _():
            v_z(o, n + 2, 1).start()

        @pl.when(jnp.logical_not(odd) & (n + 2 < last))
        def _():
            k_z(o, n + 2, -1).start()

        @pl.when(jnp.logical_not(odd) & (n + 1 <= last))
        def _():
            v_z(o, jnp.minimum(n + 2, last), -1).start()

    def ring(buf, n, o, place, at, sa, ra, sb, rb, sc, rc_, sd_, rd):
        left = lax.rem(place + NX - 1, NX)
        right = lax.rem(place + 1, NX)
        far = lax.rem(place + 2, NX)
        to_right = lambda: push(buf, o, place * quarter, quarter, sa.at[n], ra.at[n], at(1))
        to_left = lambda: push(buf, o, place * quarter, quarter, sb.at[n], rb.at[n], at(-1))
        from_left = lambda: push(buf, o, left * quarter, quarter, sa.at[n], ra.at[n], at(1))
        from_right = lambda: push(buf, o, right * quarter, quarter, sb.at[n], rb.at[n], at(-1))
        on_right = lambda: push(buf, o, left * quarter, eighth, sc.at[n], rc_.at[n], at(1))
        on_left = lambda: push(buf, o, right * quarter + eighth, eighth, sd_.at[n], rd.at[n], at(-1))
        far_left = lambda: push(buf, o, far * quarter, eighth, sc.at[n], rc_.at[n], at(1))
        far_right = lambda: push(buf, o, far * quarter + eighth, eighth, sd_.at[n], rd.at[n], at(-1))
        return to_right, to_left, from_left, from_right, on_right, on_left, far_left, far_right

    def x_ring(n, o):
        return ring(kb, n, o, x, at_x, xa_s, xa_r, xb_s, xb_r, xc_s, xc_r, xd_s, xd_r)

    def y_ring(n, o):
        return ring(vb, n, o, y, at_y, ya_s, ya_r, yb_s, yb_r, yc_s, yc_r, yd_s, yd_r)

    def arrive(n):
        o = origin(n)
        k_z(o, n, 1).wait_recv()
        v_z(o, n, 1).wait_recv()
        forward_z(n, o)
        xr, yr = x_ring(n, o), y_ring(n, o)
        xr[0]().start()
        yr[0]().start()
        xr[1]().start()
        yr[1]().start()

    def relay(n):
        o = origin(n)
        xr, yr = x_ring(n, o), y_ring(n, o)
        xr[2]().wait_recv()
        xr[4]().start()
        xr[3]().wait_recv()
        xr[5]().start()
        yr[2]().wait_recv()
        yr[4]().start()
        yr[3]().wait_recv()
        yr[5]().start()

    def settle(n):
        o = origin(n)
        xr, yr = x_ring(n, o), y_ring(n, o)
        xr[6]().wait_recv()
        xr[7]().wait_recv()
        yr[6]().wait_recv()
        yr[7]().wait_recv()

    def drain(n, carry):
        o = origin(n)
        k_z(o, n, 1).wait_send()
        v_z(o, n, 1).wait_send()
        xr, yr = x_ring(n, o), y_ring(n, o)
        for r in (xr, yr):
            r[0]().wait_send()
            r[1]().wait_send()
            r[4]().wait_send()
            r[5]().wait_send()
        return carry

    slot_rows = 4 * gr

    def attend(n):
        o = origin(n)
        for blk in range(2):
            r0_ = pl.ds(pl.multiple_of((o * 2 + blk) * slot_rows, slot_rows), slot_rows)
            sl = pl.ds((o * 2 + blk) * 4, 4)
            cube = (4, gr, HD)
            for h in range(heads):
                cols = slice(h * HD, (h + 1) * HD)
                kk = kb[o, blk * rows:(blk + 1) * rows, cols]
                vv = vb[o, blk * rows:(blk + 1) * rows, cols]
                sc = dot_nt(qg[r0_, cols], kk) * scale
                peak = jnp.max(sc, axis=-1, keepdims=True)
                e = jnp.exp(sc - peak)
                tot = jnp.sum(e, axis=-1, keepdims=True)
                p = e / tot
                dp = dot_nt(mg[r0_, cols], vv)
                delta = jnp.sum(p * dp, axis=-1, keepdims=True)
                pb = p.astype(BF16)
                dsb = (p * (dp - delta)).astype(BF16)
                po[sl, :, cols] = dot_nn(pb, vv).reshape(cube)
                ab = dot_nn(jnp.concatenate([dsb, pb], axis=0), kk)
                da[sl, :, cols] = ab[:slot_rows].reshape(cube)
                db[sl, :, cols] = ab[slot_rows:].reshape(cube)
                ls[sl, :, cols] = jnp.broadcast_to(peak + jnp.log(tot), (slot_rows, HD)).reshape(cube)
                dl[sl, :, cols] = jnp.broadcast_to(delta, (slot_rows, HD)).reshape(cube)

    def pick():
        lane = lax.rem(lax.broadcasted_iota(jnp.int32, (1, 2 * rows), 1), gr)
        c0 = jnp.concatenate([codes[0, 0:1, :], codes[1, 0:1, :]], axis=1) * gr + lane
        c1 = jnp.concatenate([codes[0, 1:2, :], codes[1, 1:2, :]], axis=1) * gr + lane
        chunk = 128

        def step(i, carry):
            r = lax.broadcasted_iota(jnp.int32, (chunk, 2 * rows), 0) + i * chunk
            hot = jnp.where((r == c0) | (r == c1), 1.0, 0.0).astype(BF16)
            at = pl.ds(pl.multiple_of(i * chunk, chunk), chunk)
            qg[at, :] = dot_nn(hot, qs[...]).astype(BF16)
            mg[at, :] = dot_nn(hot, md[...]).astype(BF16)
            return carry

        lax.fori_loop(0, qg.shape[0] // chunk, step, 0)

    def local(i, carry):
        at = pl.ds(pl.multiple_of(i * rows, rows), rows)
        ri = lax.broadcasted_iota(jnp.int32, (rows, rows), 0)
        ci = lax.broadcasted_iota(jnp.int32, (rows, rows), 1)
        for h in range(heads):
            cols = slice(h * HD, (h + 1) * HD)
            kk, vv = ks[at, cols], vs[at, cols]
            sc = jnp.where(ri >= ci, dot_nt(qs[at, cols], kk) * scale, -1e30)
            e = jnp.exp(sc - jnp.max(sc, axis=-1, keepdims=True))
            p = e / jnp.sum(e, axis=-1, keepdims=True)
            o = dot_nn(p.astype(BF16), vv)
            ld = ((1.0 - gx[0:1, cols]) * gs[at, cols].astype(F32)).astype(BF16)
            delta = jnp.sum(ld.astype(F32) * o, axis=-1, keepdims=True)
            ds = (p * (dot_nt(ld, vv) - delta)).astype(BF16)
            lo[at, cols] = o
            ldq[at, cols] = dot_nn(ds, kk) * scale
        return carry

    got_swap(0)
    k_z(z, 1, 1).start()
    k_z(z, 2, -1).start()
    got_swap(1)
    v_z(z, 1, 1).start()
    v_z(z, 2, -1).start()

    got_swap(2)
    got_swap(3)
    pltpu.make_async_remote_copy(
        src_ref=codes.at[other], dst_ref=codes.at[other],
        send_sem=swap_s.at[6], recv_sem=swap_r.at[6], device_id=sib, device_id_type=MESH,
    ).wait_recv()
    to_smem = pltpu.make_async_copy(codes, codes_sm, loc.at[6])
    to_smem.start()
    md[...] = (gx[0:1, :] * gs[...].astype(F32)).astype(BF16)
    pick()
    to_smem.wait()
    got_swap(4)
    got_swap(5)

    relay_lag, settle_lag = 2, 4

    def turn(n, carry):
        @pl.when(n <= last)
        def _():
            arrive(n)

        @pl.when(n == 2)
        def _():
            lax.fori_loop(0, 2, local, 0)

        @pl.when((n > relay_lag) & (n - relay_lag <= last))
        def _():
            relay(n - relay_lag)

        @pl.when(n > settle_lag)
        def _():
            settle(n - settle_lag)

        @pl.when(n >= settle_lag)
        def _():
            attend(n - settle_lag)

        return carry

    lax.fori_loop(1, last + settle_lag + 1, turn, 0)

    def blend(g, base, at, second):
        d0, d1 = codes_sm[base, 0, g * gr], codes_sm[base, 1, g * gr]
        l0, l1 = ls[d0], ls[d1]
        peak = jnp.maximum(l0, l1)
        e0, e1 = jnp.exp(l0 - peak), jnp.exp(l1 - peak)
        inv = 1.0 / (e0 + e1)
        s0, s1 = e0 * inv, e1 * inv
        mo = s0 * po[d0] + s1 * po[d1]
        own_rows = slice(gr, 2 * gr) if second else slice(0, gr)
        prod = md[at, :].astype(F32)[own_rows] * mo
        delta = jnp.concatenate(
            [
                jnp.broadcast_to(
                    jnp.sum(prod[:, h * HD:(h + 1) * HD], axis=-1, keepdims=True), (gr, HD)
                )
                for h in range(heads)
            ],
            axis=1,
        )
        dq = s0 * (da[d0] + (dl[d0] - delta) * db[d0])
        dq = dq + s1 * (da[d1] + (dl[d1] - delta) * db[d1])
        return mo, dq * scale

    def mix(i, acc):
        base = i // (groups // 2)
        base = jnp.where(base == 0, other, c)
        g = lax.rem(i, groups // 2) * 2
        at = pl.ds(pl.multiple_of(base * rows + g * gr, 2 * gr), 2 * gr)
        ma, qa = blend(g, base, at, False)
        mb, qb = blend(g + 1, base, at, True)
        mo = jnp.concatenate([ma, mb], axis=0)
        dq = jnp.concatenate([qa, qb], axis=0)
        gate = gx[0:1, :]
        loc_o = lo[at, :]
        so[at, :] = (gate * mo + (1.0 - gate) * loc_o).astype(BF16)
        sd[at, :] = (ldq[at, :] + dq).astype(BF16)
        t = gs[at, :].astype(F32) * (mo - loc_o)
        return acc + t[:gr] + t[gr:]

    acc = jnp.zeros((gr, half), F32)
    acc = lax.fori_loop(0, groups // 2, mix, acc)
    back = []
    for i, (stage, result) in enumerate(((so, out_hbm), (sd, dq_hbm))):
        cp = pltpu.make_async_remote_copy(
            src_ref=stage.at[sib_rows], dst_ref=result.at[:, mine],
            send_sem=res_s.at[i], recv_sem=res_r.at[i], device_id=sib, device_id_type=MESH,
        )
        cp.start()
        back.append(cp)
    acc = lax.fori_loop(groups // 2, groups, mix, acc)
    keep = []
    for i, (stage, result) in enumerate(((so, out_hbm), (sd, dq_hbm))):
        cp = pltpu.make_async_copy(stage.at[my_rows], result.at[:, mine], loc.at[i])
        cp.start()
        keep.append(cp)

    lane = lax.broadcasted_iota(jnp.int32, (8, HD), 1)
    term = jnp.zeros((8, HD), F32)
    for j in range(heads):
        cols = slice(j * HD, (j + 1) * HD)
        tot = jnp.sum(jnp.sum(acc[:, cols], axis=1, keepdims=True), axis=0, keepdims=True)
        gate = gx[:, cols]
        val = jnp.broadcast_to(tot, (8, HD)) * gate * (1.0 - gate)
        term = jnp.where(lane == c * heads + j, val, term)
    term = term * (1.0 / math.sqrt(total_tokens))

    def exchange(buf, place, steps, at, send, recv):
        size = buf.shape[0]

        def make(step):
            return pltpu.make_async_remote_copy(
                src_ref=buf.at[place], dst_ref=buf.at[place],
                send_sem=send.at[step], recv_sem=recv.at[step],
                device_id=at(step), device_id_type=MESH,
            )

        def start(step, carry):
            make(step).start()
            return carry

        def wait(step, carry):
            src = lax.rem(place + size - step, size)
            pltpu.make_async_remote_copy(
                src_ref=buf.at[src], dst_ref=buf.at[src],
                send_sem=send.at[step], recv_sem=recv.at[step],
                device_id=at(step), device_id_type=MESH,
            ).wait_recv()
            make(step).wait_send()
            return carry

        lax.fori_loop(1, steps + 1, start, 0)
        lax.fori_loop(1, steps + 1, wait, 0)
        out = buf[0]
        for i in range(1, size):
            out = out + buf[i]
        return out

    rc[c] = term
    term = exchange(rc, c, 1, lambda step: sib, rc_s, rc_r)
    rx[x] = term
    term = exchange(rx, x, NX - 1, at_x, rx_s, rx_r)
    ry[y] = term
    term = exchange(ry, y, NX - 1, at_y, ry_s, ry_r)
    rz[z] = term
    term = exchange(rz, z, nz - 1, at_z, rz_s, rz_r)
    gg_ref[...] = term

    for cp in keep:
        cp.wait()
    for i, result in enumerate((out_hbm, dq_hbm)):
        pltpu.make_async_remote_copy(
            src_ref=so.at[my_rows], dst_ref=result.at[:, theirs],
            send_sem=res_s.at[i], recv_sem=res_r.at[i], device_id=sib, device_id_type=MESH,
        ).wait_recv()
        back[i].wait_send()
    for cp in swaps:
        cp.wait_send()
    code_swap.wait_send()
    lax.fori_loop(1, nz, drain, 0)


def body(total_tokens, query, key, value, mem_key, mem_value, block_ids, gate_logit, d_out):
    rows, width = query.shape
    half = width // 2
    nz = lax.axis_size("mem") // 2
    gr = rows // block_ids.shape[0]
    slots = 2 * nz * 4 * gr
    dma = pltpu.SemaphoreType.DMA
    any_ = pl.BlockSpec(memory_space=pl.ANY)
    vmem = pl.BlockSpec(memory_space=pltpu.VMEM)
    smem = pl.BlockSpec(memory_space=pltpu.SMEM)
    heads = width // HD
    scratch = (
        [pltpu.VMEM((nz, 2 * rows, half), BF16)] * 2
        + [pltpu.VMEM((2 * rows, half), BF16)] * 5
        + [pltpu.VMEM((slots, half), BF16)] * 2
        + [pltpu.VMEM((slots // gr, gr, half), F32)] * 5
        + [pltpu.VMEM((2 * rows, half), F32)] * 2
        + [pltpu.VMEM((2 * rows, half), BF16)] * 2
        + [pltpu.VMEM((8, half), F32)]
        + [pltpu.VMEM((2, 8, rows), jnp.int32), pltpu.SMEM((2, 8, rows), jnp.int32)]
        + [pltpu.VMEM((size, 8, HD), F32) for size in (2, NX, NX, nz)]
        + [dma((7,)), dma((7,)), dma((7,)), dma((2,)), dma((2,))]
        + [dma((nz,))] * 20
        + [dma((size,)) for size in (2, 2, NX, NX, NX, NX, nz, nz)]
    )
    out, d_query, gate = pl.pallas_call(
        functools.partial(kernel, nz, total_tokens),
        out_shape=(
            jax.ShapeDtypeStruct((rows, width), BF16),
            jax.ShapeDtypeStruct((rows, width), BF16),
            jax.ShapeDtypeStruct((8, HD), F32),
        ),
        in_specs=[any_] * 6 + [vmem, smem],
        out_specs=(any_, any_, vmem),
        scratch_shapes=scratch,
        compiler_params=pltpu.CompilerParams(
            collective_id=0, has_side_effects=True, vmem_limit_bytes=58 * 1024 * 1024
        ),
    )(query, key, value, mem_key, mem_value, d_out, block_ids, gate_logit)
    return out, d_query, gate[0, :heads]


def solution(mesh):
    tokens = P(("seq", "mem"), None)

    def run(query, *rest):
        return jax.shard_map(
            functools.partial(body, query.shape[0]),
            mesh=mesh,
            in_specs=(tokens, tokens, tokens, P("mem", None), P("mem", None), tokens, P(), tokens),
            out_specs=(tokens, tokens, P()),
            check_vma=False,
        )(query, *rest)

    return run
```

```python
import functools
import math

import jax
import jax.numpy as jnp
from jax import lax
from jax.experimental import pallas as pl
from jax.experimental.pallas import tpu as pltpu
from jax.sharding import PartitionSpec as P

NX = 4
ROW = 2 * NX
HD = 128
QUARTER = 96
EIGHTH = QUARTER // 2
RING = NX * QUARTER
MESH = pl.DeviceIdType.MESH
F32 = jnp.float32
BF16 = jnp.bfloat16


def dot_nt(a, b):
    return lax.dot_general(a, b, (((1,), (1,)), ((), ())), preferred_element_type=F32)


def dot_nn(a, b):
    return jnp.dot(a, b, preferred_element_type=F32)


def row_sum(a):
    return jnp.sum(a, axis=-1, keepdims=True)


def kernel(
    nz, total_tokens,
    q_hbm, k_hbm, v_hbm, mk_hbm, mv_hbm, d_hbm, ids_ref, gl_ref,
    out_hbm, dq_hbm, gg_ref,
    kv, qs, gs, md, qg, mg, po, da, db, ls, dl,
    qh, kh, vh, dh, lo, ldq, lacc, rm, rq, so, sd, fo, fq, gx, codes, codes_sm, rr, ry, rz,
    loc, swap_s, swap_r,
    q_s, q_r, d_s, d_r, c_s, c_r, m_s, m_r, g_s, g_r,
    zk_s, zk_r, zv_s, zv_r,
    ya_s, ya_r, yb_s, yb_r, yc_s, yc_r, yd_s, yd_r,
    rr_s, rr_r, ry_s, ry_r, rz_s, rz_r,
):
    rows, width = q_hbm.shape
    wide = width // ROW
    mine_h = wide // HD
    heads = width // HD
    groups = ids_ref.shape[0]
    gr = rows // groups
    zrows = 4 * rows - RING
    scale = HD ** -0.5

    s = lax.axis_index("seq")
    m = lax.axis_index("mem")
    x, y = lax.rem(s, NX), s // NX
    z, c = m // 2, lax.rem(m, 2)
    r = x * 2 + c

    def at_row(step):
        p = lax.rem(r + step + ROW, ROW)
        return (y * NX + p // 2, z * 2 + lax.rem(p, 2))

    def at_y(step):
        return (lax.rem(y + step + NX, NX) * NX + x, m)

    def at_z(step):
        return (s, lax.rem(z + step + nz, nz) * 2 + c)

    sib = (s, z * 2 + 1 - c)

    def cols_of(p):
        return pl.ds(pl.multiple_of(p * wide, wide), wide)

    def rows_of(p):
        return pl.ds(pl.multiple_of(p * rows, rows), rows)

    own_k = kv.at[z, rows_of(c)]
    own_v = kv.at[z, rows_of(2 + c)]
    own = [
        pltpu.make_async_copy(src, dst, loc.at[i])
        for i, (src, dst) in enumerate((
            (mk_hbm.at[:, cols_of(r)], own_k),
            (mv_hbm.at[:, cols_of(r)], own_v),
            (q_hbm, qh),
            (k_hbm, kh),
            (v_hbm, vh),
            (d_hbm, dh),
            (q_hbm.at[:, cols_of(r)], qs.at[rows_of(r)]),
            (d_hbm.at[:, cols_of(r)], gs.at[rows_of(r)]),
        ))
    ]
    for cp in own:
        cp.start()

    barrier = pltpu.get_barrier_semaphore()

    def greet(dev):
        pl.semaphore_signal(barrier, inc=1, device_id=dev, device_id_type=MESH)

    for step in range(1, ROW):
        greet(at_row(step))
    for step in (1, -1):
        greet(at_y(step))
        greet(at_z(step))

    a0 = jnp.broadcast_to(ids_ref[:, 0:1], (groups, rows))
    a1 = jnp.broadcast_to(ids_ref[:, 1:2], (groups, rows))
    g_row = lax.broadcasted_iota(jnp.int32, (groups, rows), 0)
    g_tok = lax.broadcasted_iota(jnp.int32, (groups, rows), 1) // gr
    zero = jnp.zeros((groups, rows), jnp.int32)
    here = g_row == g_tok
    i0 = jnp.sum(jnp.where(here, a0, zero), axis=0, keepdims=True)
    i1 = jnp.sum(jnp.where(here, a1, zero), axis=0, keepdims=True)
    one = zero + 1
    earlier = g_row < g_tok
    r0 = jnp.sum(jnp.where(earlier & ((a0 == i0) | (a1 == i0)), one, zero), axis=0, keepdims=True)
    r1 = jnp.sum(jnp.where(earlier & ((a0 == i1) | (a1 == i1)), one, zero), axis=0, keepdims=True)
    code0 = i0 * (2 * ROW) + r * 2 + r0
    code1 = i1 * (2 * ROW) + r * 2 + r1
    first = lax.broadcasted_iota(jnp.int32, (8, rows), 0) == 0
    codes[r] = jnp.where(first, jnp.broadcast_to(code0, (8, rows)), jnp.broadcast_to(code1, (8, rows)))

    for j in range(heads):
        logit = jnp.full((8, HD), gl_ref[j], F32)
        gx[:, j * HD:(j + 1) * HD] = 1.0 / (1.0 + jnp.exp(-logit))

    pl.semaphore_wait(barrier, ROW - 1 + 4)

    swaps = [
        pltpu.make_async_remote_copy(
            src_ref=src.at[:, cols_of(x * 2 + 1 - c)], dst_ref=dst,
            send_sem=swap_s.at[i], recv_sem=swap_r.at[i], device_id=sib, device_id_type=MESH,
        )
        for i, (src, dst) in enumerate(((mk_hbm, own_k), (mv_hbm, own_v)))
    ]
    for cp in swaps:
        cp.start()

    def row_copy(src, dst, send, recv, step):
        return pltpu.make_async_remote_copy(
            src_ref=src, dst_ref=dst, send_sem=send.at[step], recv_sem=recv.at[step],
            device_id=at_row(step), device_id_type=MESH,
        )

    def to_row(step):
        p = lax.rem(r + step, ROW)
        return (
            row_copy(codes.at[r], codes.at[r], c_s, c_r, step),
            row_copy(q_hbm.at[:, cols_of(p)], qs.at[rows_of(r)], q_s, q_r, step),
            row_copy(d_hbm.at[:, cols_of(p)], gs.at[rows_of(r)], d_s, d_r, step),
        )

    def from_row(step):
        p = lax.rem(r + ROW - step, ROW)
        return (
            row_copy(codes.at[p], codes.at[p], c_s, c_r, step),
            row_copy(q_hbm.at[:, cols_of(p)], qs.at[rows_of(p)], q_s, q_r, step),
            row_copy(d_hbm.at[:, cols_of(p)], gs.at[rows_of(p)], d_s, d_r, step),
        )

    def push(o, row, count, send, recv, dev):
        here_ = kv.at[o, pl.ds(pl.multiple_of(row, 16), count)]
        return pltpu.make_async_remote_copy(
            src_ref=here_, dst_ref=here_, send_sem=send, recv_sem=recv, device_id=dev, device_id_type=MESH,
        )

    def k_z(o, j, step):
        return push(o, y * QUARTER, QUARTER, zk_s.at[j], zk_r.at[j], at_z(step))

    def v_z(o, j, step):
        return push(o, RING, zrows, zv_s.at[j], zv_r.at[j], at_z(step))

    def origin(n):
        away = (n + 1) // 2
        return lax.rem(z + nz + jnp.where(lax.rem(n, 2) == 1, -away, away), nz)

    last = nz - 1

    def forward_k(n, o):
        odd = lax.rem(n, 2) == 1

        @pl.when(odd & (n + 2 <= last))
        def _():
            k_z(o, n + 2, 1).start()

        @pl.when(jnp.logical_not(odd) & (n + 2 < last))
        def _():
            k_z(o, n + 2, -1).start()

    def forward_v(n, o):
        odd = lax.rem(n, 2) == 1

        @pl.when(odd & (n + 2 < last))
        def _():
            v_z(o, n + 2, 1).start()

        @pl.when(jnp.logical_not(odd) & (n + 1 <= last))
        def _():
            v_z(o, jnp.minimum(n + 2, last), -1).start()

    left = lax.rem(y + NX - 1, NX)
    right = lax.rem(y + 1, NX)
    far = lax.rem(y + 2, NX)

    def to_right(n, o):
        return push(o, y * QUARTER, QUARTER, ya_s.at[n], ya_r.at[n], at_y(1))

    def to_left(n, o):
        return push(o, y * QUARTER, QUARTER, yb_s.at[n], yb_r.at[n], at_y(-1))

    def from_left(n, o):
        return push(o, left * QUARTER, QUARTER, ya_s.at[n], ya_r.at[n], at_y(1))

    def from_right(n, o):
        return push(o, right * QUARTER, QUARTER, yb_s.at[n], yb_r.at[n], at_y(-1))

    def on_right(n, o):
        return push(o, left * QUARTER, EIGHTH, yc_s.at[n], yc_r.at[n], at_y(1))

    def on_left(n, o):
        return push(o, right * QUARTER + EIGHTH, EIGHTH, yd_s.at[n], yd_r.at[n], at_y(-1))

    def far_left(n, o):
        return push(o, far * QUARTER, EIGHTH, yc_s.at[n], yc_r.at[n], at_y(1))

    def far_right(n, o):
        return push(o, far * QUARTER + EIGHTH, EIGHTH, yd_s.at[n], yd_r.at[n], at_y(-1))

    def arrive(n):
        o = origin(n)
        k_z(o, n, 1).wait_recv()
        forward_k(n, o)
        to_right(n, o).start()
        to_left(n, o).start()
        v_z(o, n, 1).wait_recv()
        forward_v(n, o)

    def relay(n):
        o = origin(n)
        from_left(n, o).wait_recv()
        on_right(n, o).start()
        from_right(n, o).wait_recv()
        on_left(n, o).start()

    def settle(n):
        o = origin(n)
        far_left(n, o).wait_recv()
        far_right(n, o).wait_recv()

    def drain(n, carry):
        o = origin(n)
        for cp in (k_z(o, n, 1), v_z(o, n, 1), to_right(n, o), to_left(n, o), on_right(n, o), on_left(n, o)):
            cp.wait_send()
        return carry

    my_gate = gx.at[:, cols_of(r)]
    slots_b = 2 * ROW
    srows = slots_b * gr

    def attend(n):
        o = origin(n)
        units = [(blk, h) for blk in range(2) for h in range(mine_h)]
        for part in range(0, len(units), 4):
            todo = units[part:part + 4]
            kk, vv, sc, dp = [], [], [], []
            for blk, h in todo:
                cols = slice(h * HD, (h + 1) * HD)
                kk.append(kv[o, blk * rows:(blk + 1) * rows, cols])
                vv.append(kv[o, (2 + blk) * rows:(3 + blk) * rows, cols])
            for i, (blk, h) in enumerate(todo):
                cols = slice(h * HD, (h + 1) * HD)
                sc.append(dot_nt(qg[:, o * 2 + blk, :, cols].reshape(srows, HD), kk[i]) * scale)
            for i, (blk, h) in enumerate(todo):
                cols = slice(h * HD, (h + 1) * HD)
                dp.append(dot_nt(mg[:, o * 2 + blk, :, cols].reshape(srows, HD), vv[i]))
            peak = [jnp.max(a, axis=-1, keepdims=True) for a in sc]
            e = [jnp.exp(a - b) for a, b in zip(sc, peak)]
            tot = [row_sum(a) for a in e]
            p = [a * (1.0 / b) for a, b in zip(e, tot)]
            pb = [a.astype(BF16) for a in p]
            delta = [row_sum(a * b) for a, b in zip(p, dp)]
            dsb = [(a * (b - d)).astype(BF16) for a, b, d in zip(p, dp, delta)]
            for i, (blk, h) in enumerate(todo):
                cols = slice(h * HD, (h + 1) * HD)
                sl = pl.ds((o * 2 + blk) * slots_b, slots_b)
                cube = (slots_b, gr, HD)
                po[sl, :, cols] = dot_nn(pb[i], vv[i]).reshape(cube)
                db[sl, :, cols] = dot_nn(pb[i], kk[i]).reshape(cube)
                da[sl, :, cols] = dot_nn(dsb[i], kk[i]).reshape(cube)
                ls[sl, :, cols] = jnp.broadcast_to(peak[i] + jnp.log(tot[i]), (srows, HD)).reshape(cube)
                dl[sl, :, cols] = jnp.broadcast_to(delta[i], (srows, HD)).reshape(cube)

    def pick(d, carry):
        here_ = rows_of(d)
        md[here_, :] = (my_gate[0:1, :] * gs[here_, :].astype(F32)).astype(BF16)
        lane = lax.broadcasted_iota(jnp.int32, (1, rows), 1) & (gr - 1)
        c0, c1 = codes[d, 0:1, :], codes[d, 1:2, :]
        t0 = ((c0 // (2 * ROW)) * 2 + (c0 & 1)) * gr + lane
        t1 = ((c1 // (2 * ROW)) * 2 + (c1 & 1)) * gr + lane
        count = qg.shape[1] * 2 * gr
        at = lax.broadcasted_iota(jnp.int32, (count, rows), 0)
        hot = jnp.where((at == t0) | (at == t1), 1.0, 0.0).astype(BF16)
        cube = (qg.shape[1], 2 * gr, wide)
        qg[d] = dot_nn(hot, qs[here_, :]).astype(BF16).reshape(cube)
        mg[d] = dot_nn(hot, md[here_, :]).astype(BF16).reshape(cube)
        return carry

    ahead = 4

    def local(i):
        ri = lax.broadcasted_iota(jnp.int32, (rows, rows), 0)
        ci = lax.broadcasted_iota(jnp.int32, (rows, rows), 1)
        cols = [pl.ds(pl.multiple_of(i * (ahead * HD) + h * HD, HD), HD) for h in range(ahead)]
        kk = [kh[:, a] for a in cols]
        vv = [vh[:, a] for a in cols]
        g = [dh[:, a].astype(F32) for a in cols]
        ld = [((1.0 - gx[0:1, a]) * b).astype(BF16) for a, b in zip(cols, g)]
        sc = [jnp.where(ri >= ci, dot_nt(qh[:, a], b) * scale, -1e30) for a, b in zip(cols, kk)]
        dp = [dot_nt(a, b) for a, b in zip(ld, vv)]
        e = [jnp.exp(a - jnp.max(a, axis=-1, keepdims=True)) for a in sc]
        p = [a * (1.0 / row_sum(a)) for a in e]
        o = [dot_nn(a.astype(BF16), b) for a, b in zip(p, vv)]
        delta = [row_sum(a.astype(F32) * b) for a, b in zip(ld, o)]
        ds = [(a * (b - d)).astype(BF16) for a, b, d in zip(p, dp, delta)]
        for h, a in enumerate(cols):
            lo[:, a] = o[h]
            ldq[:, a] = dot_nn(ds[h], kk[h]) * scale
            lacc[:, a] = jnp.sum((g[h] * o[h]).reshape(rows // 8, 8, HD), axis=0)

    own[0].wait()
    swap_in = [
        pltpu.make_async_remote_copy(
            src_ref=src.at[:, cols_of(r)], dst_ref=kv.at[z, rows_of(base + 1 - c)],
            send_sem=swap_s.at[i], recv_sem=swap_r.at[i], device_id=sib, device_id_type=MESH,
        )
        for i, (src, base) in enumerate(((mk_hbm, 0), (mv_hbm, 2)))
    ]
    own[1].wait()
    swap_in[0].wait_recv()
    swap_in[1].wait_recv()
    k_z(z, 1, 1).start()
    k_z(z, 2, -1).start()
    v_z(z, 1, 1).start()
    v_z(z, 2, -1).start()

    def send_row(step, carry):
        for cp in to_row(step):
            cp.start()
        return carry

    lax.fori_loop(1, ROW, send_row, 0)
    for cp in own[2:]:
        cp.wait()

    relay_lag, settle_lag, ready = 2, 4, 9

    def turn(n, carry):
        @pl.when(n <= last)
        def _():
            arrive(n)

        @pl.when((n > relay_lag) & (n - relay_lag <= last))
        def _():
            relay(n - relay_lag)

        @pl.when(n > settle_lag)
        def _():
            settle(n - settle_lag)

        @pl.when(n <= heads // ahead)
        def _():
            local(n - 1)

        @pl.when(n == ready)
        def _():
            def take(step, carry):
                for cp in from_row(step):
                    cp.wait_recv()
                return carry

            lax.fori_loop(1, ROW, take, 0)
            lax.fori_loop(0, ROW, pick, 0)
            to_smem = pltpu.make_async_copy(codes, codes_sm, loc.at[8])
            to_smem.start()
            to_smem.wait()

        def reached(t):
            return jnp.maximum(jnp.minimum(t - settle_lag + 1, 2 * (t - ready + 1)), 0)

        def step(i, carry):
            attend(i)
            return carry

        lax.fori_loop(reached(n - 1), reached(n), step, 0)
        return carry

    lax.fori_loop(1, last + settle_lag + 1, turn, 0)

    def blend(base, g, at, second):
        d0, d1 = codes_sm[base, 0, g * gr], codes_sm[base, 1, g * gr]
        l0, l1 = ls[d0], ls[d1]
        peak = jnp.maximum(l0, l1)
        e0, e1 = jnp.exp(l0 - peak), jnp.exp(l1 - peak)
        inv = 1.0 / (e0 + e1)
        s0, s1 = e0 * inv, e1 * inv
        mo = s0 * po[d0] + s1 * po[d1]
        own_rows = slice(gr, 2 * gr) if second else slice(0, gr)
        prod = md[at, :].astype(F32)[own_rows] * mo
        delta = jnp.concatenate(
            [jnp.broadcast_to(row_sum(prod[:, h * HD:(h + 1) * HD]), (gr, HD)) for h in range(mine_h)], axis=1
        )
        dq = s0 * (da[d0] + (dl[d0] - delta) * db[d0])
        dq = dq + s1 * (da[d1] + (dl[d1] - delta) * db[d1])
        return mo, dq * scale

    def give_back(p, step):
        return (
            row_copy(so.at[rows_of(p)], rm.at[:, cols_of(r)], m_s, m_r, step),
            row_copy(sd.at[rows_of(p)], rq.at[:, cols_of(r)], g_s, g_r, step),
        )

    def merge(i, acc):
        step = lax.rem(i + ROW // 2, ROW)
        base = lax.rem(r + step, ROW)

        def pair(g2, acc):
            g = g2 * 2
            at = pl.ds(pl.multiple_of(base * rows + g * gr, 2 * gr), 2 * gr)
            ma, qa = blend(base, g, at, False)
            mb, qb = blend(base, g + 1, at, True)
            mo = jnp.concatenate([ma, mb], axis=0)
            so[at, :] = mo.astype(BF16)
            sd[at, :] = jnp.concatenate([qa, qb], axis=0).astype(BF16)
            t = gs[at, :].astype(F32) * mo
            return acc + t[:gr] + t[gr:]

        acc = lax.fori_loop(0, groups // 2, pair, acc)

        @pl.when(step > 0)
        def _():
            for cp in give_back(base, step):
                cp.start()

        @pl.when(step == 0)
        def _():
            pltpu.make_async_copy(so.at[rows_of(r)], rm.at[:, cols_of(r)], loc.at[9]).start()
            pltpu.make_async_copy(sd.at[rows_of(r)], rq.at[:, cols_of(r)], loc.at[10]).start()

        return acc

    acc = lax.fori_loop(0, ROW, merge, jnp.zeros((gr, wide), F32))

    lane = lax.broadcasted_iota(jnp.int32, (8, HD), 1)
    term = jnp.zeros((8, HD), F32)
    gates = jnp.zeros((8, HD), F32)

    def spread(a):
        return jnp.broadcast_to(jnp.sum(row_sum(a), axis=0, keepdims=True), (8, HD))

    for j in range(heads):
        cols = slice(j * HD, (j + 1) * HD)
        term = jnp.where(lane == j, -spread(lacc[:, cols]), term)
        gates = jnp.where(lane == j, gx[:, cols], gates)
    for j in range(mine_h):
        term = term + jnp.where(lane == r * mine_h + j, spread(acc[:, j * HD:(j + 1) * HD]), 0.0)
    term = term * gates * (1.0 - gates) * (1.0 / math.sqrt(total_tokens))

    def exchange(buf, place, at, send, recv):
        size = buf.shape[0]

        def make(step, src):
            return pltpu.make_async_remote_copy(
                src_ref=buf.at[src], dst_ref=buf.at[src], send_sem=send.at[step], recv_sem=recv.at[step],
                device_id=at(step), device_id_type=MESH,
            )

        def start(step, carry):
            make(step, place).start()
            return carry

        def wait(step, carry):
            make(step, lax.rem(place + size - step, size)).wait_recv()
            make(step, place).wait_send()
            return carry

        lax.fori_loop(1, size, start, 0)
        lax.fori_loop(1, size, wait, 0)
        out = buf[0]
        for i in range(1, size):
            out = out + buf[i]
        return out

    rr[r] = term
    term = exchange(rr, r, at_row, rr_s, rr_r)
    ry[y] = term
    term = exchange(ry, y, at_y, ry_s, ry_r)
    rz[z] = term
    gg_ref[...] = exchange(rz, z, at_z, rz_s, rz_r)

    def taken(step, carry):
        for cp in give_back(r, step):
            cp.wait_send()
        p = lax.rem(r + ROW - step, ROW)
        row_copy(so.at[rows_of(r)], rm.at[:, cols_of(p)], m_s, m_r, step).wait_recv()
        row_copy(sd.at[rows_of(r)], rq.at[:, cols_of(p)], g_s, g_r, step).wait_recv()
        return carry

    lax.fori_loop(1, ROW, taken, 0)
    pltpu.make_async_copy(so.at[rows_of(r)], rm.at[:, cols_of(r)], loc.at[9]).wait()
    pltpu.make_async_copy(sd.at[rows_of(r)], rq.at[:, cols_of(r)], loc.at[10]).wait()

    def finish(i, carry):
        at = pl.ds(pl.multiple_of(i * 16, 16), 16)
        gate = gx[0:1, :]
        fo[at, :] = (gate * rm[at, :].astype(F32) + (1.0 - gate) * lo[at, :]).astype(BF16)
        fq[at, :] = (ldq[at, :] + rq[at, :].astype(F32)).astype(BF16)
        return carry

    lax.fori_loop(0, rows // 16, finish, 0)
    keep = [
        pltpu.make_async_copy(fo, out_hbm, loc.at[0]),
        pltpu.make_async_copy(fq, dq_hbm, loc.at[1]),
    ]
    for cp in keep:
        cp.start()

    for cp in swaps:
        cp.wait_send()

    def sent(step, carry):
        for cp in to_row(step):
            cp.wait_send()
        return carry

    lax.fori_loop(1, ROW, sent, 0)
    lax.fori_loop(1, nz, drain, 0)
    for cp in keep:
        cp.wait()


def body(total_tokens, query, key, value, mem_key, mem_value, block_ids, gate_logit, d_out):
    rows, width = query.shape
    wide = width // ROW
    nz = lax.axis_size("mem") // 2
    gr = rows // block_ids.shape[0]
    blocks = 2 * nz
    dma = pltpu.SemaphoreType.DMA
    any_ = pl.BlockSpec(memory_space=pl.ANY)
    vmem = pl.BlockSpec(memory_space=pltpu.VMEM)
    smem = pl.BlockSpec(memory_space=pltpu.SMEM)
    heads = width // HD
    scratch = (
        [pltpu.VMEM((nz, 4 * rows, wide), BF16)]
        + [pltpu.VMEM((ROW * rows, wide), BF16)] * 3
        + [pltpu.VMEM((ROW, blocks, 2 * gr, wide), BF16)] * 2
        + [pltpu.VMEM((blocks * 2 * ROW, gr, wide), F32)] * 5
        + [pltpu.VMEM((rows, width), BF16)] * 4
        + [pltpu.VMEM((rows, width), F32)] * 2
        + [pltpu.VMEM((8, width), F32)]
        + [pltpu.VMEM((rows, width), BF16)] * 2
        + [pltpu.VMEM((ROW * rows, wide), BF16)] * 2
        + [pltpu.VMEM((rows, width), BF16)] * 2
        + [pltpu.VMEM((8, width), F32)]
        + [pltpu.VMEM((ROW, 8, rows), jnp.int32), pltpu.SMEM((ROW, 8, rows), jnp.int32)]
        + [pltpu.VMEM((size, 8, HD), F32) for size in (ROW, NX, nz)]
        + [dma((11,)), dma((2,)), dma((2,))]
        + [dma((ROW,))] * 10
        + [dma((nz,))] * 12
        + [dma((size,)) for size in (ROW, ROW, NX, NX, nz, nz)]
    )
    out, d_query, gate = pl.pallas_call(
        functools.partial(kernel, nz, total_tokens),
        out_shape=(
            jax.ShapeDtypeStruct((rows, width), BF16),
            jax.ShapeDtypeStruct((rows, width), BF16),
            jax.ShapeDtypeStruct((8, HD), F32),
        ),
        in_specs=[any_] * 6 + [vmem, smem],
        out_specs=(any_, any_, vmem),
        scratch_shapes=scratch,
        compiler_params=pltpu.CompilerParams(
            collective_id=0, has_side_effects=True, vmem_limit_bytes=56 * 1024 * 1024
        ),
    )(query, key, value, mem_key, mem_value, d_out, block_ids, gate_logit)
    return out, d_query, gate[0, :heads]


def solution(mesh):
    tokens = P(("seq", "mem"), None)

    def run(query, *rest):
        return jax.shard_map(
            functools.partial(body, query.shape[0]),
            mesh=mesh,
            in_specs=(tokens, tokens, tokens, P("mem", None), P("mem", None), tokens, P(), tokens),
            out_specs=(tokens, tokens, P()),
            check_vma=False,
        )(query, *rest)

    return run
```

```python
import functools
import math

import jax
import jax.numpy as jnp
from jax import lax
from jax.experimental import pallas as pl
from jax.experimental.pallas import tpu as pltpu
from jax.sharding import PartitionSpec as P

HD = 128
MESH = pl.DeviceIdType.MESH
F32 = jnp.float32
BF16 = jnp.bfloat16


def dot_nt(a, b):
    return lax.dot_general(a, b, (((1,), (1,)), ((), ())), preferred_element_type=F32)


def dot_nn(a, b):
    return jnp.dot(a, b, preferred_element_type=F32)


def row_sum(a):
    return jnp.sum(a, axis=-1, keepdims=True)


def kernel(
    nz, total_tokens,
    q_hbm, k_hbm, v_hbm, mk_hbm, mv_hbm, d_hbm, ids_ref, gl_ref,
    rm, rq, lo_hbm, ldq_hbm, gg_ref,
    kv, qs, gs, md, qg, po, da, db, ls, dl,
    qh, kh, vh, dh, lo, ldq, lacc, so, sd, gx, codes, codes_sm, rr, ry, rz,
    loc,
    q_s, q_r, d_s, d_r, c_s, c_r, m_s, m_r, g_s, g_r,
    z_s, z_r, b_s, b_r,
    rr_s, rr_r, ry_s, ry_r, rz_s, rz_r,
):
    rows, width = q_hbm.shape
    heads = width // HD
    plane = qg.shape[0]
    groups = ids_ref.shape[1]
    gr = rows // groups
    scale = HD ** -0.5

    s = lax.axis_index("seq")
    m = lax.axis_index("mem")
    z, c = m // 2, lax.rem(m, 2)
    toward = 1 - 2 * c

    def at_plane(step):
        return (lax.rem(s + step, plane), m)

    def at_z(step):
        return (s, lax.rem(z + step + nz, nz) * 2 + c)

    def at_sib(step):
        return (s, z * 2 + 1 - c)

    sib = at_sib(1)

    def cols_of(p):
        return pl.ds(pl.multiple_of(p * HD, HD), HD)

    def rows_of(p):
        return pl.ds(pl.multiple_of(p * rows, rows), rows)

    own = [
        pltpu.make_async_copy(src, dst, loc.at[i])
        for i, (src, dst) in enumerate((
            (mk_hbm.at[:, cols_of(s)], kv.at[z, c, 0]),
            (mv_hbm.at[:, cols_of(s)], kv.at[z, c, 1]),
            (q_hbm, qh),
            (d_hbm, dh),
            (k_hbm, kh),
            (v_hbm, vh),
        ))
    ]
    for cp in own:
        cp.start()

    barrier = pltpu.get_barrier_semaphore()

    def greet(dev):
        pl.semaphore_signal(barrier, inc=1, device_id=dev, device_id_type=MESH)

    greet(sib)
    for step in (1, -1, 2, -2):
        greet(at_z(step))

    def greet_plane(step, carry):
        greet(at_plane(step))
        return carry

    lax.fori_loop(1, plane, greet_plane, 0)

    g_row = lax.broadcasted_iota(jnp.int32, (groups, rows), 0)
    g_tok = lax.broadcasted_iota(jnp.int32, (groups, rows), 1) // gr
    zero = jnp.zeros((groups, rows), jnp.int32)
    a0, a1, i0, i1 = zero, zero, zero, zero
    for g in range(groups):
        b0, b1 = ids_ref[0, g], ids_ref[1, g]
        a0, a1 = jnp.where(g_row == g, b0, a0), jnp.where(g_row == g, b1, a1)
        i0, i1 = jnp.where(g_tok == g, b0, i0), jnp.where(g_tok == g, b1, i1)
    one = zero + 1
    earlier = g_row < g_tok
    r0 = jnp.sum(jnp.where(earlier & ((a0 == i0) | (a1 == i0)), one, zero), axis=0, keepdims=True)
    r1 = jnp.sum(jnp.where(earlier & ((a0 == i1) | (a1 == i1)), one, zero), axis=0, keepdims=True)
    code0 = i0[0:1] * (2 * plane) + s * 2 + r0
    code1 = i1[0:1] * (2 * plane) + s * 2 + r1
    first = lax.broadcasted_iota(jnp.int32, (8, rows), 0) == 0
    codes[s] = jnp.where(first, jnp.broadcast_to(code0, (8, rows)), jnp.broadcast_to(code1, (8, rows)))

    for j in range(heads):
        logit = jnp.full((8, HD), gl_ref[j], F32)
        gx[:, j * HD:(j + 1) * HD] = 1.0 / (1.0 + jnp.exp(-logit))

    pl.semaphore_wait(barrier, plane - 1 + 5)

    def plane_copy(src, dst, send, recv, step):
        return pltpu.make_async_remote_copy(
            src_ref=src, dst_ref=dst, send_sem=send.at[step], recv_sem=recv.at[step],
            device_id=at_plane(step), device_id_type=MESH,
        )

    def to_plane(step):
        p = lax.rem(s + step, plane)
        return (
            plane_copy(codes.at[s], codes.at[s], c_s, c_r, step),
            plane_copy(qh.at[:, cols_of(p)], qs.at[rows_of(s)], q_s, q_r, step),
            plane_copy(dh.at[:, cols_of(p)], gs.at[rows_of(s)], d_s, d_r, step),
        )

    def from_plane(step):
        p = lax.rem(s + plane - step, plane)
        return (
            plane_copy(codes.at[p], codes.at[p], c_s, c_r, step),
            plane_copy(qh.at[:, cols_of(p)], qs.at[rows_of(p)], q_s, q_r, step),
            plane_copy(dh.at[:, cols_of(p)], gs.at[rows_of(p)], d_s, d_r, step),
        )

    last = nz - 1

    def origin(n):
        away = (n + 1) // 2 * toward
        return lax.rem(z + nz + jnp.where(lax.rem(n, 2) == 1, -away, away), nz)

    def along_z(o, n, step):
        return pltpu.make_async_remote_copy(
            src_ref=kv.at[o, c], dst_ref=kv.at[o, c], send_sem=z_s.at[n], recv_sem=z_r.at[n],
            device_id=at_z(step), device_id_type=MESH,
        )

    def across(o, who):
        return pltpu.make_async_remote_copy(
            src_ref=kv.at[o, who], dst_ref=kv.at[o, who], send_sem=b_s.at[o], recv_sem=b_r.at[o],
            device_id=sib, device_id_type=MESH,
        )

    def spread_z(o, hops):
        @pl.when(2 * hops + 3 <= last)
        def _():
            along_z(o[0], 2 * hops + 3, 2 * toward).start()

        @pl.when(2 * hops + 4 <= last)
        def _():
            along_z(o[1], 2 * hops + 4, -2 * toward).start()

        along_z(o[0], 2 * hops + 1, toward).start()
        along_z(o[1], 2 * hops + 2, -toward).start()

    def arrive(n):
        o = origin(n)
        along_z(o, n, 1).wait_recv()
        across(o, c).start()

    def drain(n, carry):
        along_z(z, n, 1).wait_send()
        across(origin(n), c).wait_send()
        return carry

    my_gate = gx.at[:, cols_of(s)]
    slots_b = 2 * plane
    srows = slots_b * gr

    def attend(n):
        o = origin(n)
        todo = range(2)
        at = [qg.at[:, o * 2 + blk] for blk in todo]
        kk = [kv[o, blk, 0] for blk in todo]
        vv = [kv[o, blk, 1] for blk in todo]
        sc = [dot_nt(at[i][:, :, 0:HD].reshape(srows, HD), kk[i]) * scale for i in todo]
        dp = [dot_nt(at[i][:, :, HD:2 * HD].reshape(srows, HD), vv[i]) for i in todo]
        peak = [jnp.max(a, axis=-1, keepdims=True) for a in sc]
        e = [jnp.exp(a - b) for a, b in zip(sc, peak)]
        tot = [row_sum(a) for a in e]
        p = [a * (1.0 / b) for a, b in zip(e, tot)]
        pb = [a.astype(BF16) for a in p]
        delta = [row_sum(a * b) for a, b in zip(p, dp)]
        dsb = [(a * (b - d)).astype(BF16) for a, b, d in zip(p, dp, delta)]
        cube = (slots_b, gr, HD)
        for i in todo:
            sl = pl.ds((o * 2 + i) * slots_b, slots_b)
            po[sl] = dot_nn(pb[i], vv[i]).reshape(cube)
            db[sl] = dot_nn(pb[i], kk[i]).reshape(cube)
            da[sl] = dot_nn(dsb[i], kk[i]).reshape(cube)
            ls[sl] = jnp.broadcast_to(peak[i] + jnp.log(tot[i]), (srows, HD)).reshape(cube)
            dl[sl] = jnp.broadcast_to(delta[i], (srows, HD)).reshape(cube)

    def pick(d, carry):
        here_ = rows_of(d)
        md[here_, :] = (my_gate[0:1, :] * gs[here_, :].astype(F32)).astype(BF16)
        lane = lax.broadcasted_iota(jnp.int32, (1, rows), 1) & (gr - 1)
        c0, c1 = codes[d, 0:1, :], codes[d, 1:2, :]
        t0 = ((c0 // (2 * plane)) * 2 + (c0 & 1)) * gr + lane
        t1 = ((c1 // (2 * plane)) * 2 + (c1 & 1)) * gr + lane
        count = qg.shape[1] * 2 * gr
        at = lax.broadcasted_iota(jnp.int32, (count, rows), 0)
        hot = jnp.where((at == t0) | (at == t1), 1.0, 0.0).astype(BF16)
        both = jnp.concatenate([qs[here_, :], md[here_, :]], axis=1)
        qg[d] = dot_nn(hot, both).astype(BF16).reshape(qg.shape[1], 2 * gr, 2 * HD)
        return carry

    ahead = 4

    def local(i):
        ri = lax.broadcasted_iota(jnp.int32, (rows, rows), 0)
        ci = lax.broadcasted_iota(jnp.int32, (rows, rows), 1)
        cols = [pl.ds(pl.multiple_of(i * (ahead * HD) + h * HD, HD), HD) for h in range(ahead)]
        kk = [kh[:, a] for a in cols]
        vv = [vh[:, a] for a in cols]
        g = [dh[:, a].astype(F32) for a in cols]
        ld = [((1.0 - gx[0:1, a]) * b).astype(BF16) for a, b in zip(cols, g)]
        sc = [jnp.where(ri >= ci, dot_nt(qh[:, a], b) * scale, -1e30) for a, b in zip(cols, kk)]
        dp = [dot_nt(a, b) for a, b in zip(ld, vv)]
        e = [jnp.exp(a - jnp.max(a, axis=-1, keepdims=True)) for a in sc]
        p = [a * (1.0 / row_sum(a)) for a in e]
        o = [dot_nn(a.astype(BF16), b) for a, b in zip(p, vv)]
        delta = [row_sum(a.astype(F32) * b) for a, b in zip(ld, o)]
        ds = [(a * (b - d)).astype(BF16) for a, b, d in zip(p, dp, delta)]
        for h, a in enumerate(cols):
            lo[:, a] = (1.0 - gx[0:1, a]) * o[h]
            ldq[:, a] = dot_nn(ds[h], kk[h]) * scale
            lacc[:, a] = jnp.sum((g[h] * o[h]).reshape(rows // 8, 8, HD), axis=0)

    home = [
        pltpu.make_async_copy(lo, lo_hbm, loc.at[0]),
        pltpu.make_async_copy(ldq, ldq_hbm, loc.at[1]),
    ]

    own[0].wait()
    own[1].wait()
    spread_z((z, z), 0)
    across(z, c).start()
    own[2].wait()
    own[3].wait()

    def send_plane(step, carry):
        for cp in to_plane(step):
            cp.start()
        return carry

    lax.fori_loop(1, plane, send_plane, 0)
    keep = [
        pltpu.make_async_copy(qh.at[:, cols_of(s)], qs.at[rows_of(s)], loc.at[6]),
        pltpu.make_async_copy(dh.at[:, cols_of(s)], gs.at[rows_of(s)], loc.at[7]),
    ]
    for cp in keep:
        cp.start()
    own[4].wait()
    own[5].wait()

    turns = nz // 4
    ready = 3

    def turn(t, carry):
        far = 4 * t - 1

        @pl.when(t < turns)
        def _():
            a, b = origin(far), origin(far + 1)
            along_z(a, far, 1).wait_recv()
            along_z(b, far + 1, 1).wait_recv()
            spread_z((a, b), 2 * t)
            across(a, c).start()
            across(b, c).start()

        @pl.when(t <= turns)
        def _():
            arrive(far - 2)
            arrive(far - 1)

        @pl.when(t == turns)
        def _():
            arrive(far)

        @pl.when(t <= 2)
        def _():
            local(2 * t - 2)
            local(2 * t - 1)

        @pl.when(t == 2)
        def _():
            for cp in home:
                cp.start()

        @pl.when(t == ready)
        def _():
            def take(step, carry):
                for cp in from_plane(step):
                    cp.wait_recv()
                return carry

            lax.fori_loop(1, plane, take, 0)
            for cp in keep:
                cp.wait()
            lax.fori_loop(0, plane, pick, 0)
            to_smem = pltpu.make_async_copy(codes, codes_sm, loc.at[8])
            to_smem.start()
            to_smem.wait()

        def reached(t):
            return jnp.maximum(jnp.minimum(jnp.minimum(4 * t - 2, nz), 7 * (t - ready + 1)), 0)

        def step(i, carry):
            across(origin(i), 1 - c).wait_recv()
            attend(i)
            return carry

        lax.fori_loop(reached(t - 1), reached(t), step, 0)
        return carry

    lax.fori_loop(1, turns + 2, turn, 0)

    def blend(base, g0, count):
        rows_ = pl.ds(pl.multiple_of(base * rows + g0 * gr, 2 * gr), count * gr)
        gs_ = [g0 + i for i in range(count)]
        d0 = [codes_sm[base, 0, g * gr] for g in gs_]
        d1 = [codes_sm[base, 1, g * gr] for g in gs_]
        l0, l1 = [ls[d] for d in d0], [ls[d] for d in d1]
        peak = [jnp.maximum(a, b) for a, b in zip(l0, l1)]
        e0 = [jnp.exp(a - b) for a, b in zip(l0, peak)]
        e1 = [jnp.exp(a - b) for a, b in zip(l1, peak)]
        inv = [1.0 / (a + b) for a, b in zip(e0, e1)]
        s0 = [a * b for a, b in zip(e0, inv)]
        s1 = [a * b for a, b in zip(e1, inv)]
        mo = [a * po[i] + b * po[j] for a, b, i, j in zip(s0, s1, d0, d1)]
        grads = md[rows_, :].astype(F32)
        prod = [grads[i * gr:(i + 1) * gr] * a for i, a in enumerate(mo)]
        delta = [row_sum(a) for a in prod]
        dq = [a * (da[i] + (dl[i] - d) * db[i]) for a, i, d in zip(s0, d0, delta)]
        dq = [q + a * (da[i] + (dl[i] - d) * db[i]) for q, a, i, d in zip(dq, s1, d1, delta)]
        so[rows_, :] = (my_gate[0:1, :] * jnp.concatenate(mo, axis=0)).astype(BF16)
        sd[rows_, :] = (scale * jnp.concatenate(dq, axis=0)).astype(BF16)
        draw = gs[rows_, :].astype(F32)
        return sum([draw[i * gr:(i + 1) * gr] * a for i, a in enumerate(mo)])

    def give_back(p, step):
        return (
            plane_copy(so.at[rows_of(p)], rm.at[:, cols_of(s)], m_s, m_r, step),
            plane_copy(sd.at[rows_of(p)], rq.at[:, cols_of(s)], g_s, g_r, step),
        )

    own_back = [
        pltpu.make_async_copy(so.at[rows_of(s)], rm.at[:, cols_of(s)], loc.at[9]),
        pltpu.make_async_copy(sd.at[rows_of(s)], rq.at[:, cols_of(s)], loc.at[10]),
    ]
    together = 16

    def merge(i, acc):
        step = lax.rem(i + plane // 2, plane)
        base = lax.rem(s + step, plane)

        def some(i, acc):
            return acc + blend(base, i * together, together)

        acc = lax.fori_loop(0, groups // together, some, acc)

        @pl.when(step > 0)
        def _():
            for cp in give_back(base, step):
                cp.start()

        @pl.when(step == 0)
        def _():
            for cp in own_back:
                cp.start()

        return acc

    acc = lax.fori_loop(0, plane, merge, jnp.zeros((gr, HD), F32))

    lane = lax.broadcasted_iota(jnp.int32, (8, HD), 1)
    term = jnp.zeros((8, HD), F32)
    gates = jnp.zeros((8, HD), F32)

    def spread(a):
        return jnp.broadcast_to(jnp.sum(row_sum(a), axis=0, keepdims=True), (8, HD))

    for j in range(heads):
        cols = slice(j * HD, (j + 1) * HD)
        term = jnp.where(lane == j, -spread(lacc[:, cols]), term)
        gates = jnp.where(lane == j, gx[:, cols], gates)
    term = term + jnp.where(lane == s, spread(acc), 0.0)
    term = term * gates * (1.0 - gates) * (1.0 / math.sqrt(total_tokens))

    def exchange(buf, place, at, send, recv):
        size = buf.shape[0]

        def make(step, src):
            return pltpu.make_async_remote_copy(
                src_ref=buf.at[src], dst_ref=buf.at[src], send_sem=send.at[step], recv_sem=recv.at[step],
                device_id=at(step), device_id_type=MESH,
            )

        def start(step, carry):
            make(step, place).start()
            return carry

        def wait(step, carry):
            make(step, lax.rem(place + size - step, size)).wait_recv()
            make(step, place).wait_send()
            return carry

        lax.fori_loop(1, size, start, 0)
        lax.fori_loop(1, size, wait, 0)
        out = buf[0]
        for i in range(1, size):
            out = out + buf[i]
        return out

    rz[z] = term
    term = exchange(rz, z, at_z, rz_s, rz_r)
    ry[c] = term
    term = exchange(ry, c, at_sib, ry_s, ry_r)
    rr[s] = term
    gg_ref[...] = exchange(rr, s, at_plane, rr_s, rr_r)

    def taken(step, carry):
        p = lax.rem(s + plane - step, plane)
        for cp in give_back(s, step):
            cp.wait_send()
        plane_copy(so.at[rows_of(s)], rm.at[:, cols_of(p)], m_s, m_r, step).wait_recv()
        plane_copy(sd.at[rows_of(s)], rq.at[:, cols_of(p)], g_s, g_r, step).wait_recv()
        return carry

    lax.fori_loop(1, plane, taken, 0)
    for cp in own_back:
        cp.wait()

    def sent(step, carry):
        for cp in to_plane(step):
            cp.wait_send()
        return carry

    lax.fori_loop(1, plane, sent, 0)
    across(z, c).wait_send()
    lax.fori_loop(1, nz, drain, 0)
    for cp in home:
        cp.wait()


def body(total_tokens, query, key, value, mem_key, mem_value, block_ids, gate_logit, d_out):
    rows, width = query.shape
    nz, plane = lax.axis_size("mem") // 2, lax.axis_size("seq")
    gr = rows // block_ids.shape[0]
    blocks = 2 * nz
    dma = pltpu.SemaphoreType.DMA
    any_ = pl.BlockSpec(memory_space=pl.ANY)
    vmem = pl.BlockSpec(memory_space=pltpu.VMEM)
    smem = pl.BlockSpec(memory_space=pltpu.SMEM)
    heads = width // HD
    scratch = (
        [pltpu.VMEM((nz, 2, 2, rows, HD), BF16)]
        + [pltpu.VMEM((plane * rows, HD), BF16)] * 3
        + [pltpu.VMEM((plane, blocks, 2 * gr, 2 * HD), BF16)]
        + [pltpu.VMEM((blocks * 2 * plane, gr, HD), F32)] * 5
        + [pltpu.VMEM((rows, width), BF16)] * 4
        + [pltpu.VMEM((rows, width), F32)] * 2
        + [pltpu.VMEM((8, width), F32)]
        + [pltpu.VMEM((plane * rows, HD), BF16)] * 2
        + [pltpu.VMEM((8, width), F32)]
        + [pltpu.VMEM((plane, 8, rows), jnp.int32), pltpu.SMEM((plane, 8, rows), jnp.int32)]
        + [pltpu.VMEM((size, 8, HD), F32) for size in (plane, 2, nz)]
        + [dma((11,))]
        + [dma((plane,))] * 10
        + [dma((nz,))] * 4
        + [dma((size,)) for size in (plane, plane, 2, 2, nz, nz)]
    )
    mem_out, mem_dq, local_out, local_dq, gate = pl.pallas_call(
        functools.partial(kernel, nz, total_tokens),
        out_shape=(
            jax.ShapeDtypeStruct((rows, width), BF16),
            jax.ShapeDtypeStruct((rows, width), BF16),
            jax.ShapeDtypeStruct((rows, width), F32),
            jax.ShapeDtypeStruct((rows, width), F32),
            jax.ShapeDtypeStruct((8, HD), F32),
        ),
        in_specs=[any_] * 6 + [smem, smem],
        out_specs=(any_, any_, any_, any_, vmem),
        scratch_shapes=scratch,
        compiler_params=pltpu.CompilerParams(
            collective_id=0, has_side_effects=True, vmem_limit_bytes=56 * 1024 * 1024
        ),
    )(query, key, value, mem_key, mem_value, d_out, block_ids.T, gate_logit)
    out = (mem_out.astype(F32) + local_out).astype(BF16)
    d_query = (mem_dq.astype(F32) + local_dq).astype(BF16)
    return out, d_query, gate[0, :heads]


def solution(mesh):
    tokens = P(("seq", "mem"), None)

    def run(query, *rest):
        return jax.shard_map(
            functools.partial(body, query.shape[0]),
            mesh=mesh,
            in_specs=(tokens, tokens, tokens, P("mem", None), P("mem", None), tokens, P(), tokens),
            out_specs=(tokens, tokens, P()),
            check_vma=False,
        )(query, *rest)

    return run
```

```python
import functools
import math

import jax
import jax.numpy as jnp
from jax import lax
from jax.experimental import pallas as pl
from jax.experimental.pallas import tpu as pltpu
from jax.sharding import PartitionSpec as P

HD = 128
MESH = pl.DeviceIdType.MESH
F32 = jnp.float32
BF16 = jnp.bfloat16


def dot_nt(a, b):
    return lax.dot_general(a, b, (((1,), (1,)), ((), ())), preferred_element_type=F32)


def dot_nn(a, b):
    return jnp.dot(a, b, preferred_element_type=F32)


def row_sum(a):
    return jnp.sum(a, axis=-1, keepdims=True)


def kernel(
    nz, total_tokens,
    q_hbm, k_hbm, v_hbm, mk_hbm, mv_hbm, d_hbm, ids_ref, gl_ref,
    rm, rq, lo_hbm, ldq_hbm, gg_ref,
    kv, qs, gs, md, qg, mg, hots, pf, sh0, sh1, dt, po, da, db, ls, dl,
    qh, kh, vh, dh, lo, ldq, lacc, so, sd, gx, codes, codes_sm, rr, ry, rz,
    loc,
    q_s, q_r, d_s, d_r, c_s, c_r, m_s, m_r, g_s, g_r,
    z_s, z_r, b_s, b_r,
    rr_s, rr_r, ry_s, ry_r, rz_s, rz_r,
):
    rows, width = q_hbm.shape
    heads = width // HD
    plane = qg.shape[0]
    groups = ids_ref.shape[1]
    gr = rows // groups
    scale = HD ** -0.5

    s = lax.axis_index("seq")
    m = lax.axis_index("mem")
    z, c = m // 2, lax.rem(m, 2)
    toward = 1 - 2 * c

    def at_plane(step):
        return (lax.rem(s + step, plane), m)

    def at_z(step):
        return (s, lax.rem(z + step + nz, nz) * 2 + c)

    def at_sib(step):
        return (s, z * 2 + 1 - c)

    sib = at_sib(1)

    def cols_of(p):
        return pl.ds(pl.multiple_of(p * HD, HD), HD)

    def rows_of(p):
        return pl.ds(pl.multiple_of(p * rows, rows), rows)

    own = [
        pltpu.make_async_copy(src, dst, loc.at[i])
        for i, (src, dst) in enumerate((
            (mk_hbm.at[:, cols_of(s)], kv.at[z, c, 0]),
            (mv_hbm.at[:, cols_of(s)], kv.at[z, c, 1]),
            (q_hbm, qh),
            (d_hbm, dh),
            (k_hbm, kh),
            (v_hbm, vh),
        ))
    ]
    for cp in own:
        cp.start()

    barrier = pltpu.get_barrier_semaphore()

    def greet(dev):
        pl.semaphore_signal(barrier, inc=1, device_id=dev, device_id_type=MESH)

    greet(sib)
    for step in (1, -1, 2, -2):
        greet(at_z(step))

    def greet_plane(step, carry):
        greet(at_plane(step))
        return carry

    lax.fori_loop(1, plane, greet_plane, 0)

    pl.semaphore_wait(barrier, plane - 1 + 5)

    def plane_copy(src, dst, send, recv, step):
        return pltpu.make_async_remote_copy(
            src_ref=src, dst_ref=dst, send_sem=send.at[step], recv_sem=recv.at[step],
            device_id=at_plane(step), device_id_type=MESH,
        )

    def queries(step, p, q):
        return (
            plane_copy(codes.at[q], codes.at[q], c_s, c_r, step),
            plane_copy(qh.at[:, cols_of(p)], qs.at[rows_of(q)], q_s, q_r, step),
        )

    def grads(step, p, q):
        return (plane_copy(dh.at[:, cols_of(p)], gs.at[rows_of(q)], d_s, d_r, step),)

    def each_peer(make, sending, act):
        def go(step, carry):
            if sending:
                copies = make(step, lax.rem(s + step, plane), s)
            else:
                copies = make(step, s, lax.rem(s + plane - step, plane))
            for cp in copies:
                act(cp)
            return carry

        lax.fori_loop(1, plane, go, 0)

    last = nz - 1

    def origin(n):
        away = (n + 1) // 2 * toward
        return lax.rem(z + nz + jnp.where(lax.rem(n, 2) == 1, -away, away), nz)

    def along_z(o, n, step, part):
        return pltpu.make_async_remote_copy(
            src_ref=kv.at[o, c, part], dst_ref=kv.at[o, c, part],
            send_sem=z_s.at[part * nz + n], recv_sem=z_r.at[part * nz + n],
            device_id=at_z(step), device_id_type=MESH,
        )

    def across(o, who):
        return pltpu.make_async_remote_copy(
            src_ref=kv.at[o, who], dst_ref=kv.at[o, who], send_sem=b_s.at[o], recv_sem=b_r.at[o],
            device_id=sib, device_id_type=MESH,
        )

    def spread_z(o, hops, part):
        @pl.when(2 * hops + 3 <= last)
        def _():
            along_z(o[0], 2 * hops + 3, 2 * toward, part).start()

        @pl.when(2 * hops + 4 <= last)
        def _():
            along_z(o[1], 2 * hops + 4, -2 * toward, part).start()

        along_z(o[0], 2 * hops + 1, toward, part).start()
        along_z(o[1], 2 * hops + 2, -toward, part).start()

    def arrive(n):
        o = origin(n)
        along_z(o, n, 1, 0).wait_recv()
        along_z(o, n, 1, 1).wait_recv()
        across(o, c).start()

    def drain(n, carry):
        along_z(z, n, 1, 0).wait_send()
        along_z(z, n, 1, 1).wait_send()
        across(origin(n), c).wait_send()
        return carry

    my_gate = gx.at[:, cols_of(s)]
    slots_b = 2 * plane
    srows = slots_b * gr

    cube = (slots_b, gr, HD)
    def blocks_of(planes):
        return [(o, blk) for o in planes for blk in range(2)]

    def forward(planes):
        todo = blocks_of(planes)
        sc = [dot_nt(qg[:, o * 2 + blk].reshape(srows, HD), kv[o, blk, 0]) * scale for o, blk in todo]
        peak = [jnp.max(a, axis=-1, keepdims=True) for a in sc]
        e = [jnp.exp(a - b) for a, b in zip(sc, peak)]
        tot = [row_sum(a) for a in e]
        p = [a * (1.0 / b) for a, b in zip(e, tot)]
        for i, (o, blk) in enumerate(todo):
            sl = pl.ds((o * 2 + blk) * slots_b, slots_b)
            pf[o * 2 + blk] = p[i]
            ls[sl] = jnp.broadcast_to(peak[i] + jnp.log(tot[i]), (srows, HD)).reshape(cube)
            po[sl] = dot_nn(p[i].astype(BF16), kv[o, blk, 1]).reshape(cube)

    def backward(planes):
        todo = blocks_of(planes)
        dp = [dot_nt(mg[:, o * 2 + blk].reshape(srows, HD), kv[o, blk, 1]) for o, blk in todo]
        p = [pf[o * 2 + blk] for o, blk in todo]
        delta = [row_sum(a * b) for a, b in zip(p, dp)]
        dsb = [(a * (b - d)).astype(BF16) for a, b, d in zip(p, dp, delta)]
        for i, (o, blk) in enumerate(todo):
            sl = pl.ds((o * 2 + blk) * slots_b, slots_b)
            dl[sl] = jnp.broadcast_to(delta[i], (srows, HD)).reshape(cube)
            db[sl] = dot_nn(p[i].astype(BF16), kv[o, blk, 0]).reshape(cube)
            da[sl] = dot_nn(dsb[i], kv[o, blk, 0]).reshape(cube)

    per_pick = 4

    def pick_q(i, carry):
        lane = lax.broadcasted_iota(jnp.int32, (1, rows), 1) & (gr - 1)
        count = qg.shape[1] * 2 * gr
        at = lax.broadcasted_iota(jnp.int32, (count, rows), 0)
        hot = []
        for j in range(per_pick):
            d = i * per_pick + j
            c0, c1 = codes[d, 0:1, :], codes[d, 1:2, :]
            t0 = ((c0 // (2 * plane)) * 2 + (c0 & 1)) * gr + lane
            t1 = ((c1 // (2 * plane)) * 2 + (c1 & 1)) * gr + lane
            hot.append(jnp.where((at == t0) | (at == t1), 1.0, 0.0).astype(BF16))
        for j in range(per_pick):
            d = i * per_pick + j
            hots[d] = hot[j]
            qg[d] = dot_nn(hot[j], qs[rows_of(d), :]).astype(BF16).reshape(qg.shape[1], 2 * gr, HD)
        return carry

    def pick_d(i, carry):
        for j in range(per_pick):
            d = i * per_pick + j
            here_ = rows_of(d)
            gated = (my_gate[0:1, :] * gs[here_, :].astype(F32)).astype(BF16)
            md[here_, :] = gated
            mg[d] = dot_nn(hots[d], gated).astype(BF16).reshape(mg.shape[1], 2 * gr, HD)
        return carry

    ahead = 4

    def local(i):
        ri = lax.broadcasted_iota(jnp.int32, (rows, rows), 0)
        ci = lax.broadcasted_iota(jnp.int32, (rows, rows), 1)
        cols = [pl.ds(pl.multiple_of(i * (ahead * HD) + h * HD, HD), HD) for h in range(ahead)]
        kk = [kh[:, a] for a in cols]
        vv = [vh[:, a] for a in cols]
        g = [dh[:, a].astype(F32) for a in cols]
        ld = [((1.0 - gx[0:1, a]) * b).astype(BF16) for a, b in zip(cols, g)]
        sc = [jnp.where(ri >= ci, dot_nt(qh[:, a], b) * scale, -1e30) for a, b in zip(cols, kk)]
        dp = [dot_nt(a, b) for a, b in zip(ld, vv)]
        e = [jnp.exp(a - jnp.max(a, axis=-1, keepdims=True)) for a in sc]
        p = [a * (1.0 / row_sum(a)) for a in e]
        o = [dot_nn(a.astype(BF16), b) for a, b in zip(p, vv)]
        delta = [row_sum(a.astype(F32) * b) for a, b in zip(ld, o)]
        ds = [(a * (b - d)).astype(BF16) for a, b, d in zip(p, dp, delta)]
        for h, a in enumerate(cols):
            lo[:, a] = (1.0 - gx[0:1, a]) * o[h]
            ldq[:, a] = dot_nn(ds[h], kk[h]) * scale
            lacc[:, a] = jnp.sum((g[h] * o[h]).reshape(rows // 8, 8, HD), axis=0)

    home = [
        pltpu.make_async_copy(lo, lo_hbm, loc.at[0]),
        pltpu.make_async_copy(ldq, ldq_hbm, loc.at[1]),
    ]

    for part in range(2):
        own[part].wait()
        spread_z((z, z), 0, part)
    across(z, c).start()
    g_row = lax.broadcasted_iota(jnp.int32, (groups, rows), 0)
    g_tok = lax.broadcasted_iota(jnp.int32, (groups, rows), 1) // gr
    zero = jnp.zeros((groups, rows), jnp.int32)
    a0, a1, i0, i1 = zero, zero, zero, zero
    for g in range(groups):
        b0, b1 = ids_ref[0, g], ids_ref[1, g]
        a0, a1 = jnp.where(g_row == g, b0, a0), jnp.where(g_row == g, b1, a1)
        i0, i1 = jnp.where(g_tok == g, b0, i0), jnp.where(g_tok == g, b1, i1)
    one = zero + 1
    earlier = g_row < g_tok
    r0 = jnp.sum(jnp.where(earlier & ((a0 == i0) | (a1 == i0)), one, zero), axis=0, keepdims=True)
    r1 = jnp.sum(jnp.where(earlier & ((a0 == i1) | (a1 == i1)), one, zero), axis=0, keepdims=True)
    code0 = i0[0:1] * (2 * plane) + s * 2 + r0
    code1 = i1[0:1] * (2 * plane) + s * 2 + r1
    first = lax.broadcasted_iota(jnp.int32, (8, rows), 0) == 0
    codes[s] = jnp.where(first, jnp.broadcast_to(code0, (8, rows)), jnp.broadcast_to(code1, (8, rows)))

    for j in range(heads):
        logit = jnp.full((8, HD), gl_ref[j], F32)
        gx[:, j * HD:(j + 1) * HD] = 1.0 / (1.0 + jnp.exp(-logit))

    own[2].wait()
    own[3].wait()

    each_peer(queries, True, lambda cp: cp.start())
    each_peer(grads, True, lambda cp: cp.start())
    keep = [
        pltpu.make_async_copy(qh.at[:, cols_of(s)], qs.at[rows_of(s)], loc.at[6]),
        pltpu.make_async_copy(dh.at[:, cols_of(s)], gs.at[rows_of(s)], loc.at[7]),
    ]
    for cp in keep:
        cp.start()
    own[4].wait()
    own[5].wait()

    turns = nz // 4
    ready, ready_d = 2, 3

    def back_pair(i, carry):
        backward([origin(2 * i), origin(2 * i + 1)])
        return carry

    def turn(t, carry):
        far = 4 * t - 1

        @pl.when(t < turns)
        def _():
            a, b = origin(far), origin(far + 1)
            for part in range(2):
                along_z(a, far, 1, part).wait_recv()
                along_z(b, far + 1, 1, part).wait_recv()
                spread_z((a, b), 2 * t, part)
            across(a, c).start()
            across(b, c).start()

        @pl.when(t <= turns)
        def _():
            arrive(far - 2)
            arrive(far - 1)

        @pl.when(t == turns)
        def _():
            arrive(far)

        @pl.when(t <= 2)
        def _():
            for i in range(heads // ahead // 2):
                local((t - 1) * (heads // ahead // 2) + i)

        @pl.when(t == 2)
        def _():
            for cp in home:
                cp.start()

        @pl.when(t == ready)
        def _():
            each_peer(queries, False, lambda cp: cp.wait_recv())
            keep[0].wait()
            to_smem = pltpu.make_async_copy(codes, codes_sm, loc.at[8])
            to_smem.start()
            lax.fori_loop(0, plane // per_pick, pick_q, 0)
            to_smem.wait()

        @pl.when(t == ready_d)
        def _():
            each_peer(grads, False, lambda cp: cp.wait_recv())
            keep[1].wait()
            lax.fori_loop(0, plane // per_pick, pick_d, 0)

        def reached(t):
            return jnp.maximum(jnp.minimum(jnp.minimum(2 * t - 1, nz // 2), 4 * (t - ready + 1)), 0)

        def step(i, carry):
            across(origin(2 * i), 1 - c).wait_recv()
            across(origin(2 * i + 1), 1 - c).wait_recv()
            forward([origin(2 * i), origin(2 * i + 1)])
            return carry

        lax.fori_loop(reached(t - 1), reached(t), step, 0)

        @pl.when(t <= turns)
        def _():
            lax.fori_loop(1 * jnp.maximum(t - ready_d, 0), 1 * jnp.maximum(t - ready_d + 1, 0), back_pair, 0)

        return carry

    lax.fori_loop(1, turns + 2, turn, 0)
    early = 1 * (turns - ready_d + 1)

    groups_ = range(groups)

    def slots_of(base):
        return (
            [codes_sm[base, 0, g * gr] for g in groups_],
            [codes_sm[base, 1, g * gr] for g in groups_],
        )

    def cut(a):
        return [a[i * gr:(i + 1) * gr] for i in groups_]

    def mix_out(base):
        at = rows_of(base)
        d0, d1 = slots_of(base)
        l0, l1 = [ls[d] for d in d0], [ls[d] for d in d1]
        peak = [jnp.maximum(a, b) for a, b in zip(l0, l1)]
        e0 = [jnp.exp(a - b) for a, b in zip(l0, peak)]
        e1 = [jnp.exp(a - b) for a, b in zip(l1, peak)]
        inv = [1.0 / (a + b) for a, b in zip(e0, e1)]
        s0 = [a * b for a, b in zip(e0, inv)]
        s1 = [a * b for a, b in zip(e1, inv)]
        mo = [a * po[i] + b * po[j] for a, b, i, j in zip(s0, s1, d0, d1)]
        prod = [a * b for a, b in zip(cut(md[at, :].astype(F32)), mo)]
        so[at, :] = (my_gate[0:1, :] * jnp.concatenate(mo, axis=0)).astype(BF16)
        sh0[at, :] = jnp.concatenate(s0, axis=0)
        sh1[at, :] = jnp.concatenate(s1, axis=0)
        dt[at, :] = jnp.concatenate([jnp.broadcast_to(row_sum(a), (gr, HD)) for a in prod], axis=0)
        return sum([a * b for a, b in zip(cut(gs[at, :].astype(F32)), mo)])

    def mix_dq(base):
        at = rows_of(base)
        d0, d1 = slots_of(base)
        delta = cut(dt[at, :])
        dq = [a * (da[i] + (dl[i] - d) * db[i]) for a, i, d in zip(cut(sh0[at, :]), d0, delta)]
        dq = [q + a * (da[i] + (dl[i] - d) * db[i]) for q, a, i, d in zip(dq, cut(sh1[at, :]), d1, delta)]
        sd[at, :] = (scale * jnp.concatenate(dq, axis=0)).astype(BF16)

    def out_back(p, q, step):
        return plane_copy(so.at[rows_of(p)], rm.at[:, cols_of(q)], m_s, m_r, step)

    def dq_back(p, q, step):
        return plane_copy(sd.at[rows_of(p)], rq.at[:, cols_of(q)], g_s, g_r, step)

    own_back = [
        pltpu.make_async_copy(so.at[rows_of(s)], rm.at[:, cols_of(s)], loc.at[9]),
        pltpu.make_async_copy(sd.at[rows_of(s)], rq.at[:, cols_of(s)], loc.at[10]),
    ]

    per_merge = 2

    def merge_out(i, acc):
        for j in range(per_merge):
            base = lax.rem(s + i * per_merge + j + plane // 2, plane)
            acc = acc + mix_out(base)
        for j in range(per_merge):
            step = lax.rem(i * per_merge + j + plane // 2, plane)
            base = lax.rem(s + step, plane)

            @pl.when(step > 0)
            def _(base=base, step=step):
                out_back(base, s, step).start()

        return acc

    acc = lax.fori_loop(0, plane // per_merge, merge_out, jnp.zeros((gr, HD), F32))
    own_back[0].start()

    lane = lax.broadcasted_iota(jnp.int32, (8, HD), 1)
    term = jnp.zeros((8, HD), F32)
    gates = jnp.zeros((8, HD), F32)

    def spread(a):
        return jnp.broadcast_to(jnp.sum(row_sum(a), axis=0, keepdims=True), (8, HD))

    for j in range(heads):
        cols = slice(j * HD, (j + 1) * HD)
        term = jnp.where(lane == j, -spread(lacc[:, cols]), term)
        gates = jnp.where(lane == j, gx[:, cols], gates)
    term = term + jnp.where(lane == s, spread(acc), 0.0)
    term = term * gates * (1.0 - gates) * (1.0 / math.sqrt(total_tokens))

    def peers(buf, place, at, send, recv):
        size = buf.shape[0]

        def make(step, src):
            return pltpu.make_async_remote_copy(
                src_ref=buf.at[src], dst_ref=buf.at[src], send_sem=send.at[step], recv_sem=recv.at[step],
                device_id=at(step), device_id_type=MESH,
            )

        def start(step, carry):
            make(step, place).start()
            return carry

        def wait(step, carry):
            make(step, lax.rem(place + size - step, size)).wait_recv()
            make(step, place).wait_send()
            return carry

        def post(a):
            buf[place] = a
            lax.fori_loop(1, size, start, 0)

        def total():
            lax.fori_loop(1, size, wait, 0)
            out = buf[0]
            for i in range(1, size):
                out = out + buf[i]
            return out

        return post, total

    post_z, total_z = peers(rz, z, at_z, rz_s, rz_r)
    post_c, total_c = peers(ry, c, at_sib, ry_s, ry_r)
    post_p, total_p = peers(rr, s, at_plane, rr_s, rr_r)
    post_z(term)

    lax.fori_loop(early, nz // 2, back_pair, 0)
    def merge_dq(i, carry):
        for j in range(per_merge):
            mix_dq(lax.rem(s + i * per_merge + j + plane // 2, plane))
        for j in range(per_merge):
            step = lax.rem(i * per_merge + j + plane // 2, plane)
            base = lax.rem(s + step, plane)

            @pl.when(step > 0)
            def _(base=base, step=step):
                dq_back(base, s, step).start()

        return carry

    lax.fori_loop(0, plane // per_merge, merge_dq, 0)
    own_back[1].start()

    post_c(total_z())
    post_p(total_c())

    each_peer(queries, True, lambda cp: cp.wait_send())
    each_peer(grads, True, lambda cp: cp.wait_send())
    across(z, c).wait_send()
    lax.fori_loop(1, nz, drain, 0)
    for cp in home:
        cp.wait()

    def taken(step, carry):
        p = lax.rem(s + plane - step, plane)
        out_back(s, s, step).wait_send()
        dq_back(s, s, step).wait_send()
        out_back(s, p, step).wait_recv()
        dq_back(s, p, step).wait_recv()
        return carry

    lax.fori_loop(1, plane, taken, 0)
    for cp in own_back:
        cp.wait()
    gg_ref[...] = total_p()


def body(total_tokens, query, key, value, mem_key, mem_value, block_ids, gate_logit, d_out):
    rows, width = query.shape
    nz, plane = lax.axis_size("mem") // 2, lax.axis_size("seq")
    gr = rows // block_ids.shape[0]
    blocks = 2 * nz
    dma = pltpu.SemaphoreType.DMA
    any_ = pl.BlockSpec(memory_space=pl.ANY)
    vmem = pl.BlockSpec(memory_space=pltpu.VMEM)
    smem = pl.BlockSpec(memory_space=pltpu.SMEM)
    heads = width // HD
    scratch = (
        [pltpu.VMEM((nz, 2, 2, rows, HD), BF16)]
        + [pltpu.VMEM((plane * rows, HD), BF16)] * 3
        + [pltpu.VMEM((plane, blocks, 2 * gr, HD), BF16)] * 2
        + [pltpu.VMEM((plane, blocks * 2 * gr, rows), BF16)]
        + [pltpu.VMEM((blocks, plane * 2 * gr, HD), F32)]
        + [pltpu.VMEM((plane * rows, HD), F32)] * 3
        + [pltpu.VMEM((blocks * 2 * plane, gr, HD), F32)] * 5
        + [pltpu.VMEM((rows, width), BF16)] * 4
        + [pltpu.VMEM((rows, width), F32)] * 2
        + [pltpu.VMEM((8, width), F32)]
        + [pltpu.VMEM((plane * rows, HD), BF16)] * 2
        + [pltpu.VMEM((8, width), F32)]
        + [pltpu.VMEM((plane, 8, rows), jnp.int32), pltpu.SMEM((plane, 8, rows), jnp.int32)]
        + [pltpu.VMEM((size, 8, HD), F32) for size in (plane, 2, nz)]
        + [dma((11,))]
        + [dma((plane,))] * 10
        + [dma((2 * nz,))] * 2
        + [dma((nz,))] * 2
        + [dma((size,)) for size in (plane, plane, 2, 2, nz, nz)]
    )
    mem_out, mem_dq, local_out, local_dq, gate = pl.pallas_call(
        functools.partial(kernel, nz, total_tokens),
        out_shape=(
            jax.ShapeDtypeStruct((rows, width), BF16),
            jax.ShapeDtypeStruct((rows, width), BF16),
            jax.ShapeDtypeStruct((rows, width), F32),
            jax.ShapeDtypeStruct((rows, width), F32),
            jax.ShapeDtypeStruct((8, HD), F32),
        ),
        in_specs=[any_] * 6 + [smem, smem],
        out_specs=(any_, any_, any_, any_, vmem),
        scratch_shapes=scratch,
        compiler_params=pltpu.CompilerParams(
            collective_id=0, has_side_effects=True, vmem_limit_bytes=56 * 1024 * 1024
        ),
    )(query, key, value, mem_key, mem_value, d_out, block_ids.T, gate_logit)
    out = (mem_out.astype(F32) + local_out).astype(BF16)
    d_query = (mem_dq.astype(F32) + local_dq).astype(BF16)
    return out, d_query, gate[0, :heads]


def solution(mesh):
    tokens = P(("seq", "mem"), None)

    def run(query, *rest):
        return jax.shard_map(
            functools.partial(body, query.shape[0]),
            mesh=mesh,
            in_specs=(tokens, tokens, tokens, P("mem", None), P("mem", None), tokens, P(), tokens),
            out_specs=(tokens, tokens, P()),
            check_vma=False,
        )(query, *rest)

    return run
```

```python
import functools
import math

import jax
import jax.numpy as jnp
from jax import lax
from jax.experimental import pallas as pl
from jax.experimental.pallas import tpu as pltpu
from jax.sharding import PartitionSpec as P

HD = 128
MESH = pl.DeviceIdType.MESH
F32 = jnp.float32
BF16 = jnp.bfloat16


def dot_nt(a, b):
    return lax.dot_general(a, b, (((1,), (1,)), ((), ())), preferred_element_type=F32)


def dot_nn(a, b):
    return jnp.dot(a, b, preferred_element_type=F32)


def row_sum(a):
    return jnp.sum(a, axis=-1, keepdims=True)


def kernel(
    nz, total_tokens,
    q_hbm, k_hbm, v_hbm, mk_hbm, mv_hbm, d_hbm, ids_ref, gl_ref,
    rm, rq, lo_hbm, ldq_hbm, gg_ref,
    kv, qs, gs, md, qg, mg, hots, pf, sh0, sh1, dt, po, da, db, ls, dl,
    qh, kh, vh, dh, lo, ldq, lacc, so, sd, gx, codes, codes_sm, rr, ry, rz,
    loc,
    q_s, q_r, d_s, d_r, c_s, c_r, m_s, m_r, g_s, g_r,
    z_s, z_r, b_s, b_r,
    rr_s, rr_r, ry_s, ry_r, rz_s, rz_r,
):
    rows, width = q_hbm.shape
    heads = width // HD
    plane = qg.shape[0]
    groups = ids_ref.shape[1]
    gr = rows // groups
    scale = HD ** -0.5

    s = lax.axis_index("seq")
    m = lax.axis_index("mem")
    z, c = m // 2, lax.rem(m, 2)
    toward = 1 - 2 * c

    def at_plane(step):
        return (lax.rem(s + step, plane), m)

    def at_z(step):
        return (s, lax.rem(z + step + nz, nz) * 2 + c)

    def at_sib(step):
        return (s, z * 2 + 1 - c)

    sib = at_sib(1)

    def cols_of(p):
        return pl.ds(pl.multiple_of(p * HD, HD), HD)

    def rows_of(p):
        return pl.ds(pl.multiple_of(p * rows, rows), rows)

    own = [
        pltpu.make_async_copy(src, dst, loc.at[i])
        for i, (src, dst) in enumerate((
            (mk_hbm.at[:, cols_of(s)], kv.at[z, c, 0]),
            (mv_hbm.at[:, cols_of(s)], kv.at[z, c, 1]),
            (q_hbm, qh),
            (d_hbm, dh),
            (k_hbm, kh),
            (v_hbm, vh),
        ))
    ]
    for cp in own:
        cp.start()

    barrier = pltpu.get_barrier_semaphore()

    def greet(dev):
        pl.semaphore_signal(barrier, inc=1, device_id=dev, device_id_type=MESH)

    greet(sib)
    for step in (1, -1, 2, -2):
        greet(at_z(step))

    def greet_plane(step, carry):
        greet(at_plane(step))
        return carry

    lax.fori_loop(1, plane, greet_plane, 0)

    pl.semaphore_wait(barrier, plane - 1 + 5)

    def plane_copy(src, dst, send, recv, step):
        return pltpu.make_async_remote_copy(
            src_ref=src, dst_ref=dst, send_sem=send.at[step], recv_sem=recv.at[step],
            device_id=at_plane(step), device_id_type=MESH,
        )

    def queries(step, p, q):
        return (
            plane_copy(codes.at[q], codes.at[q], c_s, c_r, step),
            plane_copy(qh.at[:, cols_of(p)], qs.at[rows_of(q)], q_s, q_r, step),
        )

    def grads(step, p, q):
        return (plane_copy(dh.at[:, cols_of(p)], gs.at[rows_of(q)], d_s, d_r, step),)

    def each_peer(make, sending, act):
        def go(step, carry):
            if sending:
                copies = make(step, lax.rem(s + step, plane), s)
            else:
                copies = make(step, s, lax.rem(s + plane - step, plane))
            for cp in copies:
                act(cp)
            return carry

        lax.fori_loop(1, plane, go, 0)

    last = nz - 1

    def origin(n):
        away = (n + 1) // 2 * toward
        return lax.rem(z + nz + jnp.where(lax.rem(n, 2) == 1, -away, away), nz)

    def along_z(o, n, step, part):
        return pltpu.make_async_remote_copy(
            src_ref=kv.at[o, c, part], dst_ref=kv.at[o, c, part],
            send_sem=z_s.at[part * nz + n], recv_sem=z_r.at[part * nz + n],
            device_id=at_z(step), device_id_type=MESH,
        )

    def across(o, who):
        return pltpu.make_async_remote_copy(
            src_ref=kv.at[o, who], dst_ref=kv.at[o, who], send_sem=b_s.at[o], recv_sem=b_r.at[o],
            device_id=sib, device_id_type=MESH,
        )

    def two_on(o, hops, part):
        @pl.when(2 * hops + 3 <= last)
        def _():
            along_z(o[0], 2 * hops + 3, 2 * toward, part).start()

        @pl.when(2 * hops + 4 <= last)
        def _():
            along_z(o[1], 2 * hops + 4, -2 * toward, part).start()

    def one_on(o, hops):
        for part in range(2):
            along_z(o[0], 2 * hops + 1, toward, part).start()
            along_z(o[1], 2 * hops + 2, -toward, part).start()

    def arrive(n):
        o = origin(n)
        along_z(o, n, 1, 0).wait_recv()
        along_z(o, n, 1, 1).wait_recv()
        across(o, c).start()

    def drain(n, carry):
        along_z(z, n, 1, 0).wait_send()
        along_z(z, n, 1, 1).wait_send()
        across(origin(n), c).wait_send()
        return carry

    my_gate = gx.at[:, cols_of(s)]
    slots_b = 2 * plane
    srows = slots_b * gr

    cube = (slots_b, gr, HD)
    def blocks_of(planes):
        return [(o, blk) for o in planes for blk in range(2)]

    def forward(planes):
        todo = blocks_of(planes)
        sc = [dot_nt(qg[:, o * 2 + blk].reshape(srows, HD), kv[o, blk, 0]) * scale for o, blk in todo]
        peak = [jnp.max(a, axis=-1, keepdims=True) for a in sc]
        e = [jnp.exp(a - b) for a, b in zip(sc, peak)]
        tot = [row_sum(a) for a in e]
        p = [a * (1.0 / b) for a, b in zip(e, tot)]
        for i, (o, blk) in enumerate(todo):
            sl = pl.ds((o * 2 + blk) * slots_b, slots_b)
            pf[o * 2 + blk] = p[i]
            ls[sl] = jnp.broadcast_to(peak[i] + jnp.log(tot[i]), (srows, HD)).reshape(cube)
            po[sl] = dot_nn(p[i].astype(BF16), kv[o, blk, 1]).reshape(cube)

    def backward(planes):
        todo = blocks_of(planes)
        dp = [dot_nt(mg[:, o * 2 + blk].reshape(srows, HD), kv[o, blk, 1]) for o, blk in todo]
        p = [pf[o * 2 + blk] for o, blk in todo]
        delta = [row_sum(a * b) for a, b in zip(p, dp)]
        dsb = [(a * (b - d)).astype(BF16) for a, b, d in zip(p, dp, delta)]
        for i, (o, blk) in enumerate(todo):
            sl = pl.ds((o * 2 + blk) * slots_b, slots_b)
            dl[sl] = jnp.broadcast_to(delta[i], (srows, HD)).reshape(cube)
            db[sl] = dot_nn(p[i].astype(BF16), kv[o, blk, 0]).reshape(cube)
            da[sl] = dot_nn(dsb[i], kv[o, blk, 0]).reshape(cube)

    per_pick = 4

    def pick_q(i, carry):
        lane = lax.broadcasted_iota(jnp.int32, (1, rows), 1) & (gr - 1)
        count = qg.shape[1] * 2 * gr
        at = lax.broadcasted_iota(jnp.int32, (count, rows), 0)
        hot = []
        for j in range(per_pick):
            d = i * per_pick + j
            c0, c1 = codes[d, 0:1, :], codes[d, 1:2, :]
            t0 = ((c0 // (2 * plane)) * 2 + (c0 & 1)) * gr + lane
            t1 = ((c1 // (2 * plane)) * 2 + (c1 & 1)) * gr + lane
            hot.append(jnp.where((at == t0) | (at == t1), 1.0, 0.0).astype(BF16))
        for j in range(per_pick):
            d = i * per_pick + j
            hots[d] = hot[j]
            qg[d] = dot_nn(hot[j], qs[rows_of(d), :]).astype(BF16).reshape(qg.shape[1], 2 * gr, HD)
        return carry

    def pick_d(i, carry):
        for j in range(per_pick):
            d = i * per_pick + j
            here_ = rows_of(d)
            gated = (my_gate[0:1, :] * gs[here_, :].astype(F32)).astype(BF16)
            md[here_, :] = gated
            mg[d] = dot_nn(hots[d], gated).astype(BF16).reshape(mg.shape[1], 2 * gr, HD)
        return carry

    ahead = 4

    def local(i):
        ri = lax.broadcasted_iota(jnp.int32, (rows, rows), 0)
        ci = lax.broadcasted_iota(jnp.int32, (rows, rows), 1)
        cols = [pl.ds(pl.multiple_of(i * (ahead * HD) + h * HD, HD), HD) for h in range(ahead)]
        kk = [kh[:, a] for a in cols]
        vv = [vh[:, a] for a in cols]
        g = [dh[:, a].astype(F32) for a in cols]
        ld = [((1.0 - gx[0:1, a]) * b).astype(BF16) for a, b in zip(cols, g)]
        sc = [jnp.where(ri >= ci, dot_nt(qh[:, a], b) * scale, -1e30) for a, b in zip(cols, kk)]
        dp = [dot_nt(a, b) for a, b in zip(ld, vv)]
        e = [jnp.exp(a - jnp.max(a, axis=-1, keepdims=True)) for a in sc]
        p = [a * (1.0 / row_sum(a)) for a in e]
        o = [dot_nn(a.astype(BF16), b) for a, b in zip(p, vv)]
        delta = [row_sum(a.astype(F32) * b) for a, b in zip(ld, o)]
        ds = [(a * (b - d)).astype(BF16) for a, b, d in zip(p, dp, delta)]
        for h, a in enumerate(cols):
            lo[:, a] = ((1.0 - gx[0:1, a]) * o[h]).astype(BF16)
            ldq[:, a] = (dot_nn(ds[h], kk[h]) * scale).astype(BF16)
            lacc[:, a] = jnp.sum((g[h] * o[h]).reshape(rows // 8, 8, HD), axis=0)

    home = [
        pltpu.make_async_copy(lo, lo_hbm, loc.at[0]),
        pltpu.make_async_copy(ldq, ldq_hbm, loc.at[1]),
    ]

    for part in range(2):
        own[part].wait()
        two_on((z, z), 0, part)
    one_on((z, z), 0)
    across(z, c).start()
    g_row = lax.broadcasted_iota(jnp.int32, (groups, rows), 0)
    g_tok = lax.broadcasted_iota(jnp.int32, (groups, rows), 1) // gr
    zero = jnp.zeros((groups, rows), jnp.int32)
    a0, a1, i0, i1 = zero, zero, zero, zero
    for g in range(groups):
        b0, b1 = ids_ref[0, g], ids_ref[1, g]
        a0, a1 = jnp.where(g_row == g, b0, a0), jnp.where(g_row == g, b1, a1)
        i0, i1 = jnp.where(g_tok == g, b0, i0), jnp.where(g_tok == g, b1, i1)
    one = zero + 1
    earlier = g_row < g_tok
    r0 = jnp.sum(jnp.where(earlier & ((a0 == i0) | (a1 == i0)), one, zero), axis=0, keepdims=True)
    r1 = jnp.sum(jnp.where(earlier & ((a0 == i1) | (a1 == i1)), one, zero), axis=0, keepdims=True)
    code0 = i0[0:1] * (2 * plane) + s * 2 + r0
    code1 = i1[0:1] * (2 * plane) + s * 2 + r1
    first = lax.broadcasted_iota(jnp.int32, (8, rows), 0) == 0
    codes[s] = jnp.where(first, jnp.broadcast_to(code0, (8, rows)), jnp.broadcast_to(code1, (8, rows)))

    for j in range(heads):
        logit = jnp.full((8, HD), gl_ref[j], F32)
        gx[:, j * HD:(j + 1) * HD] = 1.0 / (1.0 + jnp.exp(-logit))

    own[2].wait()
    own[3].wait()

    each_peer(queries, True, lambda cp: cp.start())
    each_peer(grads, True, lambda cp: cp.start())
    keep = [
        pltpu.make_async_copy(qh.at[:, cols_of(s)], qs.at[rows_of(s)], loc.at[6]),
        pltpu.make_async_copy(dh.at[:, cols_of(s)], gs.at[rows_of(s)], loc.at[7]),
    ]
    for cp in keep:
        cp.start()
    own[4].wait()
    own[5].wait()

    turns = nz // 4
    ready, ready_d = 2, 4

    def back_pair(i, carry):
        backward([origin(2 * i), origin(2 * i + 1)])
        return carry

    def turn(t, carry):
        far = 4 * t - 1

        @pl.when(t < turns)
        def _():
            a, b = origin(far), origin(far + 1)
            for part in range(2):
                along_z(a, far, 1, part).wait_recv()
                along_z(b, far + 1, 1, part).wait_recv()
                two_on((a, b), 2 * t, part)
            one_on((a, b), 2 * t)
            across(a, c).start()
            across(b, c).start()

        @pl.when(t <= turns)
        def _():
            arrive(far - 2)
            arrive(far - 1)

        @pl.when(t == turns)
        def _():
            arrive(far)

        @pl.when(t <= 2)
        def _():
            for i in range(heads // ahead // 2):
                local((t - 1) * (heads // ahead // 2) + i)

        @pl.when(t == 2)
        def _():
            for cp in home:
                cp.start()

        @pl.when(t == ready)
        def _():
            each_peer(queries, False, lambda cp: cp.wait_recv())
            keep[0].wait()
            to_smem = pltpu.make_async_copy(codes, codes_sm, loc.at[8])
            to_smem.start()
            lax.fori_loop(0, plane // per_pick, pick_q, 0)
            to_smem.wait()

        @pl.when(t == ready_d)
        def _():
            each_peer(grads, False, lambda cp: cp.wait_recv())
            keep[1].wait()
            lax.fori_loop(0, plane // per_pick, pick_d, 0)

        def reached(t):
            return jnp.maximum(jnp.minimum(jnp.minimum(2 * t - 1, nz // 2), 4 * (t - ready + 1)), 0)

        def step(i, carry):
            across(origin(2 * i), 1 - c).wait_recv()
            across(origin(2 * i + 1), 1 - c).wait_recv()
            forward([origin(2 * i), origin(2 * i + 1)])
            return carry

        lax.fori_loop(reached(t - 1), reached(t), step, 0)

        @pl.when(t <= turns)
        def _():
            lax.fori_loop(1 * jnp.maximum(t - ready_d, 0), 1 * jnp.maximum(t - ready_d + 1, 0), back_pair, 0)

        return carry

    lax.fori_loop(1, turns + 2, turn, 0)
    early = 1 * (turns - ready_d + 1)

    groups_ = range(groups)

    def slots_of(base):
        return (
            [codes_sm[base, 0, g * gr] for g in groups_],
            [codes_sm[base, 1, g * gr] for g in groups_],
        )

    def cut(a):
        return [a[i * gr:(i + 1) * gr] for i in groups_]

    def mix_out(base):
        at = rows_of(base)
        d0, d1 = slots_of(base)
        l0, l1 = [ls[d] for d in d0], [ls[d] for d in d1]
        peak = [jnp.maximum(a, b) for a, b in zip(l0, l1)]
        e0 = [jnp.exp(a - b) for a, b in zip(l0, peak)]
        e1 = [jnp.exp(a - b) for a, b in zip(l1, peak)]
        inv = [1.0 / (a + b) for a, b in zip(e0, e1)]
        s0 = [a * b for a, b in zip(e0, inv)]
        s1 = [a * b for a, b in zip(e1, inv)]
        mo = [a * po[i] + b * po[j] for a, b, i, j in zip(s0, s1, d0, d1)]
        prod = [a * b for a, b in zip(cut(md[at, :].astype(F32)), mo)]
        so[at, :] = (my_gate[0:1, :] * jnp.concatenate(mo, axis=0)).astype(BF16)
        sh0[at, :] = jnp.concatenate(s0, axis=0)
        sh1[at, :] = jnp.concatenate(s1, axis=0)
        dt[at, :] = jnp.concatenate([jnp.broadcast_to(row_sum(a), (gr, HD)) for a in prod], axis=0)
        return sum([a * b for a, b in zip(cut(gs[at, :].astype(F32)), mo)])

    def mix_dq(base):
        at = rows_of(base)
        d0, d1 = slots_of(base)
        delta = cut(dt[at, :])
        dq = [a * (da[i] + (dl[i] - d) * db[i]) for a, i, d in zip(cut(sh0[at, :]), d0, delta)]
        dq = [q + a * (da[i] + (dl[i] - d) * db[i]) for q, a, i, d in zip(dq, cut(sh1[at, :]), d1, delta)]
        sd[at, :] = (scale * jnp.concatenate(dq, axis=0)).astype(BF16)

    def out_back(p, q, step):
        return plane_copy(so.at[rows_of(p)], rm.at[:, cols_of(q)], m_s, m_r, step)

    def dq_back(p, q, step):
        return plane_copy(sd.at[rows_of(p)], rq.at[:, cols_of(q)], g_s, g_r, step)

    own_back = [
        pltpu.make_async_copy(so.at[rows_of(s)], rm.at[:, cols_of(s)], loc.at[9]),
        pltpu.make_async_copy(sd.at[rows_of(s)], rq.at[:, cols_of(s)], loc.at[10]),
    ]

    per_merge = 2

    def merge_out(i, acc):
        for j in range(per_merge):
            base = lax.rem(s + i * per_merge + j + plane // 2, plane)
            acc = acc + mix_out(base)
        for j in range(per_merge):
            step = lax.rem(i * per_merge + j + plane // 2, plane)
            base = lax.rem(s + step, plane)

            @pl.when(step > 0)
            def _(base=base, step=step):
                out_back(base, s, step).start()

        return acc

    acc = lax.fori_loop(0, plane // per_merge, merge_out, jnp.zeros((gr, HD), F32))
    own_back[0].start()

    lane = lax.broadcasted_iota(jnp.int32, (8, HD), 1)
    term = jnp.zeros((8, HD), F32)
    gates = jnp.zeros((8, HD), F32)

    def spread(a):
        return jnp.broadcast_to(jnp.sum(row_sum(a), axis=0, keepdims=True), (8, HD))

    for j in range(heads):
        cols = slice(j * HD, (j + 1) * HD)
        term = jnp.where(lane == j, -spread(lacc[:, cols]), term)
        gates = jnp.where(lane == j, gx[:, cols], gates)
    term = term + jnp.where(lane == s, spread(acc), 0.0)
    term = term * gates * (1.0 - gates) * (1.0 / math.sqrt(total_tokens))

    def peers(buf, place, at, send, recv):
        size = buf.shape[0]

        def make(step, src):
            return pltpu.make_async_remote_copy(
                src_ref=buf.at[src], dst_ref=buf.at[src], send_sem=send.at[step], recv_sem=recv.at[step],
                device_id=at(step), device_id_type=MESH,
            )

        def start(step, carry):
            make(step, place).start()
            return carry

        def wait(step, carry):
            make(step, lax.rem(place + size - step, size)).wait_recv()
            make(step, place).wait_send()
            return carry

        def post(a):
            buf[place] = a
            lax.fori_loop(1, size, start, 0)

        def total():
            lax.fori_loop(1, size, wait, 0)
            out = buf[0]
            for i in range(1, size):
                out = out + buf[i]
            return out

        return post, total

    post_z, total_z = peers(rz, z, at_z, rz_s, rz_r)
    post_c, total_c = peers(ry, c, at_sib, ry_s, ry_r)
    post_p, total_p = peers(rr, s, at_plane, rr_s, rr_r)
    post_z(term)

    lax.fori_loop(early, nz // 2, back_pair, 0)
    def merge_dq(i, carry):
        for j in range(per_merge):
            mix_dq(lax.rem(s + i * per_merge + j + plane // 2, plane))
        for j in range(per_merge):
            step = lax.rem(i * per_merge + j + plane // 2, plane)
            base = lax.rem(s + step, plane)

            @pl.when(step > 0)
            def _(base=base, step=step):
                dq_back(base, s, step).start()

        return carry

    lax.fori_loop(0, plane // per_merge, merge_dq, 0)
    own_back[1].start()

    post_c(total_z())
    post_p(total_c())

    each_peer(queries, True, lambda cp: cp.wait_send())
    each_peer(grads, True, lambda cp: cp.wait_send())
    across(z, c).wait_send()
    lax.fori_loop(1, nz, drain, 0)
    for cp in home:
        cp.wait()

    def taken(step, carry):
        p = lax.rem(s + plane - step, plane)
        out_back(s, s, step).wait_send()
        dq_back(s, s, step).wait_send()
        out_back(s, p, step).wait_recv()
        dq_back(s, p, step).wait_recv()
        return carry

    lax.fori_loop(1, plane, taken, 0)
    for cp in own_back:
        cp.wait()
    gg_ref[...] = total_p()


def body(total_tokens, query, key, value, mem_key, mem_value, block_ids, gate_logit, d_out):
    rows, width = query.shape
    nz, plane = lax.axis_size("mem") // 2, lax.axis_size("seq")
    gr = rows // block_ids.shape[0]
    blocks = 2 * nz
    dma = pltpu.SemaphoreType.DMA
    any_ = pl.BlockSpec(memory_space=pl.ANY)
    vmem = pl.BlockSpec(memory_space=pltpu.VMEM)
    smem = pl.BlockSpec(memory_space=pltpu.SMEM)
    heads = width // HD
    scratch = (
        [pltpu.VMEM((nz, 2, 2, rows, HD), BF16)]
        + [pltpu.VMEM((plane * rows, HD), BF16)] * 3
        + [pltpu.VMEM((plane, blocks, 2 * gr, HD), BF16)] * 2
        + [pltpu.VMEM((plane, blocks * 2 * gr, rows), BF16)]
        + [pltpu.VMEM((blocks, plane * 2 * gr, HD), F32)]
        + [pltpu.VMEM((plane * rows, HD), F32)] * 3
        + [pltpu.VMEM((blocks * 2 * plane, gr, HD), F32)] * 5
        + [pltpu.VMEM((rows, width), BF16)] * 4
        + [pltpu.VMEM((rows, width), BF16)] * 2
        + [pltpu.VMEM((8, width), F32)]
        + [pltpu.VMEM((plane * rows, HD), BF16)] * 2
        + [pltpu.VMEM((8, width), F32)]
        + [pltpu.VMEM((plane, 8, rows), jnp.int32), pltpu.SMEM((plane, 8, rows), jnp.int32)]
        + [pltpu.VMEM((size, 8, HD), F32) for size in (plane, 2, nz)]
        + [dma((11,))]
        + [dma((plane,))] * 10
        + [dma((2 * nz,))] * 2
        + [dma((nz,))] * 2
        + [dma((size,)) for size in (plane, plane, 2, 2, nz, nz)]
    )
    mem_out, mem_dq, local_out, local_dq, gate = pl.pallas_call(
        functools.partial(kernel, nz, total_tokens),
        out_shape=(
            jax.ShapeDtypeStruct((rows, width), BF16),
            jax.ShapeDtypeStruct((rows, width), BF16),
            jax.ShapeDtypeStruct((rows, width), BF16),
            jax.ShapeDtypeStruct((rows, width), BF16),
            jax.ShapeDtypeStruct((8, HD), F32),
        ),
        in_specs=[any_] * 6 + [smem, smem],
        out_specs=(any_, any_, any_, any_, vmem),
        scratch_shapes=scratch,
        compiler_params=pltpu.CompilerParams(
            collective_id=0, has_side_effects=True, vmem_limit_bytes=56 * 1024 * 1024
        ),
    )(query, key, value, mem_key, mem_value, d_out, block_ids.T, gate_logit)
    out = (mem_out.astype(F32) + local_out.astype(F32)).astype(BF16)
    d_query = (mem_dq.astype(F32) + local_dq.astype(F32)).astype(BF16)
    return out, d_query, gate[0, :heads]


def solution(mesh):
    tokens = P(("seq", "mem"), None)

    def run(query, *rest):
        return jax.shard_map(
            functools.partial(body, query.shape[0]),
            mesh=mesh,
            in_specs=(tokens, tokens, tokens, P("mem", None), P("mem", None), tokens, P(), tokens),
            out_specs=(tokens, tokens, P()),
            check_vma=False,
        )(query, *rest)

    return run
```
